128 devices in a mesh: dp: 4 (over z_lo, core), ctx: 32 (over z_hi, y, x).
Axes of the slice: x: 4, y: 4, z: 4 (z_hi: 2, z_lo: 2; z = z_hi * 2 + z_lo), core: 2. Of those that a mesh axis runs over, the one named last changes fastest.
Arguments:
- quant_input: bfloat16 [4, 4096, 2048], P('dp', 'ctx'), may hold values from -6 to 6
- input_scales: float32 [4, 4096, 16], P('dp', 'ctx'), may hold values from 0.5 to 2
- out_grad: bfloat16 [4, 4096, 2048], P('dp', 'ctx'), may hold values from -6 to 6
- filter_taps: bfloat16 [2048, 4096], P(None, 'ctx'), may hold values from -1 to 1
- skip: float32 [2048], replicated, may hold values from -1 to 1
- proj_weight: bfloat16 [2048, 2048], P(('dp', 'ctx')), may hold values from -0.125 to 0.125
Outputs:
- grad_input: bfloat16 [4, 4096, 2048], P('dp', 'ctx')
- grad_filter: float32 [2048, 4096], P('ctx', 'dp')
- grad_proj: float32 [2048, 2048], P(('dp', 'ctx'))
The draws below stay inside these ranges and needn't reach their ends.
All inputs are finite; a program needn't handle non-finite values.
Results may differ from the reference program's by a relative error of at most 0.018.
Values may be sent and summed in bfloat16 or wider, within the bound.
No kernel may reach another device: no remote copies, remote signals or barrier semaphores. Data moves between devices by JAX's collectives and lax.ppermute only.
A program may use at most 128 MiB of HBM per device.

```python
import math
import jax
import jax.numpy as jnp
from jax import lax

D = 2048
QBLOCK = 128
SEQS = 4
LENGTH = 4096


def draw_filter_taps(key, part):
    key = jax.random.fold_in(key, 11)
    rate_key, noise_key = jax.random.split(key)
    low = 0.3 / LENGTH
    high = 1.0 / 40.0
    noise = jax.random.truncated_normal(noise_key, -4.0, 4.0, (D, LENGTH), jnp.float32)
    rates = jnp.exp(jax.random.uniform(rate_key, (D, 1), jnp.float32, math.log(low), math.log(high)))
    places = jnp.arange(LENGTH, dtype=jnp.float32)[None, :]
    taps = noise * jnp.exp(-rates * places) * jnp.sqrt(-jnp.expm1(-2.0 * rates))
    return taps.astype(jnp.bfloat16)


def level_of(stream_key, dims, cuts, low, largest):
    level, own = 1.0, jax.random.fold_in(stream_key, 6)
    for position, blocks in cuts:
        heights = jnp.exp(jax.random.uniform(jax.random.fold_in(own, position), (blocks,), jnp.float32, low / len(cuts), largest / len(cuts)))
        level = level * jnp.repeat(heights, dims[position] // blocks).reshape([-1 if axis == position else 1 for axis in range(len(dims))])
    return level


def gaussian(own_key, extent, deviation, reach, cuts=(), kind=jnp.bfloat16):
    level = level_of(own_key, extent, cuts, -0.22, 0.18) if cuts else 1.0
    entries = jax.random.normal(own_key, extent, jnp.float32) * deviation * level
    return jnp.minimum(jnp.maximum(entries, -reach), reach).astype(kind)


def setup_inputs(seed: int = 0) -> dict:
    keys = jax.random.split(jax.random.key(seed), 7)
    return {
        "quant_input": gaussian(keys[0], (SEQS, LENGTH, D), 1.0, 6.0, ((0, 4), (1, 32))),
        "input_scales": jnp.clip(jnp.exp(math.log(2.0) - 1.3862944 * jax.random.uniform(keys[1], (SEQS, LENGTH, D // QBLOCK), jnp.float32) ** level_of(keys[1], (SEQS, LENGTH, D // QBLOCK), ((0, 4), (1, 32)), -0.2, 0.2)), 0.5, 2.0),
        "out_grad": gaussian(keys[2], (SEQS, LENGTH, D), 1.0, 6.0, ((0, 4), (1, 32))),
        "filter_taps": draw_filter_taps(jax.random.fold_in(keys[6], 71), 0),
        "skip": jnp.clip(jax.random.uniform(keys[4], (D,), jnp.float32, -1.0, 1.0), -1.0, 1.0),
        "proj_weight": gaussian(keys[5], (D, D), D ** -0.5, 0.125, ((0, 128),)),
    }


def reference(quant_input, input_scales, out_grad, filter_taps, skip, proj_weight):
    size = 2 * LENGTH
    filter_spec = jnp.fft.rfft(filter_taps.astype(jnp.float32), n=size, axis=1)

    def one_sequence(items):
        values, scales, cotangent = items
        signal = (values.astype(jnp.float32).reshape(LENGTH, D // QBLOCK, QBLOCK) * scales[:, :, None]).reshape(LENGTH, D).astype(jnp.bfloat16)
        dconv = lax.dot_general(cotangent, proj_weight, (((1,), (1,)), ((), ())), preferred_element_type=jnp.float32).astype(jnp.bfloat16)
        signal_t = signal.astype(jnp.float32).T
        dconv_t = dconv.astype(jnp.float32).T
        signal_spec = jnp.fft.rfft(signal_t, n=size, axis=1)
        dconv_spec = jnp.fft.rfft(dconv_t, n=size, axis=1)
        conv = (jnp.fft.irfft(filter_spec * signal_spec, n=size, axis=1)[:, :LENGTH] + skip[:, None] * signal_t).astype(jnp.bfloat16)
        grad_in = (jnp.fft.irfft(jnp.conj(filter_spec) * dconv_spec, n=size, axis=1)[:, :LENGTH] + skip[:, None] * dconv_t).astype(jnp.bfloat16)
        grad_taps = jnp.fft.irfft(jnp.conj(signal_spec) * dconv_spec, n=size, axis=1)[:, :LENGTH].astype(jnp.float32)
        grad_weight = jnp.dot(conv, cotangent, preferred_element_type=jnp.float32)
        return (grad_in.T, grad_taps, grad_weight)
    grad_input, taps, weights = lax.map(one_sequence, (quant_input, input_scales, out_grad))
    factor = 1.0 / math.sqrt(SEQS * LENGTH)
    return (grad_input, lax.optimization_barrier(jnp.sum(taps, axis=0)) * factor, lax.optimization_barrier(jnp.sum(weights, axis=0)) * factor)
```

```python
import functools, math
import jax, jax.numpy as jnp
from jax import lax
from jax.experimental import pallas as pl
from jax.experimental.pallas import tpu as pltpu

LANES = 128
GROUP = 4


def wide(taps, store):
    blocks = taps.shape[0]
    rows = lax.broadcasted_iota(jnp.int32, (LANES, LANES), 0)
    cols = lax.broadcasted_iota(jnp.int32, (LANES, LANES), 1)
    same = cols >= rows
    before = jnp.zeros((LANES, LANES), jnp.float32)
    for delta in range(blocks):
        line = jnp.broadcast_to(taps[delta : delta + 1, :], (LANES, LANES))
        turned = pltpu.roll(line, 0, 1, stride=1, stride_axis=0)
        store(delta, jnp.where(same, turned, before).astype(jnp.bfloat16))
        before = turned


def later(field, seqs):
    parts = [field]
    for step in range(1, GROUP):
        gap = jnp.zeros((step * seqs, LANES), field.dtype)
        parts.append(jnp.concatenate([gap, field[: field.shape[0] - step * seqs]], axis=0))
    return jnp.concatenate([p.astype(jnp.bfloat16) for p in parts], axis=1)


def earlier(field, seqs):
    parts = [field]
    for step in range(1, GROUP):
        gap = jnp.zeros((step * seqs, LANES), field.dtype)
        parts.append(jnp.concatenate([field[step * seqs :], gap], axis=0))
    return jnp.concatenate([p.astype(jnp.bfloat16) for p in parts], axis=1)


def conv_kernel(seqs, x_ref, h_ref, skip_ref, y_ref, m_ref, acc_ref):
    ch = pl.program_id(0)
    x = x_ref[0].astype(jnp.float32)
    rows = x.shape[0]
    def put(delta, m):
        m_ref[delta * LANES : (delta + 1) * LANES, :] = m
    wide(h_ref[0].astype(jnp.float32), put)
    moved = later(x, seqs)
    acc_ref[...] = x * skip_ref[ch]
    span = GROUP * seqs
    for k in range(rows // span):
        acc_ref[k * span :, :] += jnp.dot(
            moved[: rows - k * span], m_ref[k * GROUP * LANES : (k + 1) * GROUP * LANES, :],
            preferred_element_type=jnp.float32)
    y_ref[0] = acc_ref[...].astype(jnp.bfloat16)


def grad_kernel(seqs, scale, x_ref, d_ref, h_ref, skip_ref, gi_ref, gf_ref, m_ref, acc_ref):
    ch = pl.program_id(0)
    x = x_ref[0].astype(jnp.float32)
    dval = d_ref[0]
    d = dval.astype(jnp.float32)
    rows = x.shape[0]
    span = GROUP * seqs
    steps = rows // span
    def put(delta, m):
        m_ref[:, delta * LANES : (delta + 1) * LANES] = m
    wide(h_ref[0].astype(jnp.float32), put)
    dmoved = earlier(d, seqs)
    acc_ref[...] = d * skip_ref[ch]
    for k in range(steps):
        acc_ref[: rows - k * span, :] += lax.dot_general(
            dmoved[k * span :], m_ref[:, k * GROUP * LANES : (k + 1) * GROUP * LANES],
            (((1,), (1,)), ((), ())), preferred_element_type=jnp.float32)
    gi_ref[0] = acc_ref[...].astype(jnp.bfloat16)
    ri = lax.broadcasted_iota(jnp.int32, (LANES, LANES), 0)
    ci = lax.broadcasted_iota(jnp.int32, (LANES, LANES), 1)
    flip = (ri + ci == LANES - 1).astype(jnp.bfloat16)
    xmoved = later(jnp.dot(x_ref[0], flip, preferred_element_type=jnp.float32), seqs)
    same = ri + ci >= LANES - 1
    after = jnp.zeros((LANES, LANES), jnp.float32)
    for k in reversed(range(steps)):
        g = lax.dot_general(xmoved[: rows - k * span], dval[k * span :],
            (((0,), (0,)), ((), ())), preferred_element_type=jnp.float32)
        for v in reversed(range(GROUP)):
            here = g[v * LANES : (v + 1) * LANES]
            mixed = jnp.where(same, here, after)
            turned = pltpu.roll(mixed, 1, 1, stride=1, stride_axis=0)
            delta = k * GROUP + v
            gf_ref[0, delta : delta + 1, :] = jnp.sum(turned, axis=0, keepdims=True) * scale
            after = here


def conv_call(x, h, skip, seqs):
    chans, rows, _ = x.shape
    blocks = h.shape[1]
    return pl.pallas_call(
        functools.partial(conv_kernel, seqs), grid=(chans,),
        in_specs=[pl.BlockSpec((1, rows, LANES), lambda i: (i, 0, 0)),
                  pl.BlockSpec((1, blocks, LANES), lambda i: (i, 0, 0)),
                  pl.BlockSpec(memory_space=pltpu.SMEM)],
        out_specs=pl.BlockSpec((1, rows, LANES), lambda i: (i, 0, 0)),
        out_shape=jax.ShapeDtypeStruct(x.shape, jnp.bfloat16),
        scratch_shapes=[pltpu.VMEM((blocks * LANES, LANES), jnp.bfloat16), pltpu.VMEM((rows, LANES), jnp.float32)],
        compiler_params=pltpu.CompilerParams(vmem_limit_bytes=32 << 20),
    )(x, h, skip)


def grad_call(x, d, h, skip, seqs, scale):
    chans, rows, _ = x.shape
    blocks = h.shape[1]
    big = pl.BlockSpec((1, rows, LANES), lambda i: (i, 0, 0))
    small = pl.BlockSpec((1, blocks, LANES), lambda i: (i, 0, 0))
    return pl.pallas_call(
        functools.partial(grad_kernel, seqs, scale), grid=(chans,),
        in_specs=[big, big, small, pl.BlockSpec(memory_space=pltpu.SMEM)],
        out_specs=[big, small],
        out_shape=[jax.ShapeDtypeStruct(x.shape, jnp.bfloat16), jax.ShapeDtypeStruct((chans, blocks, LANES), jnp.float32)],
        scratch_shapes=[pltpu.VMEM((LANES, blocks * LANES), jnp.bfloat16), pltpu.VMEM((rows, LANES), jnp.float32)],
        compiler_params=pltpu.CompilerParams(vmem_limit_bytes=32 << 20),
    )(x, d, h, skip)


from jax.sharding import PartitionSpec as P


def on_device(quant_input, input_scales, out_grad, filter_taps, skip, proj_weight):
    tokens, width = quant_input.shape[1:]
    ctx = lax.axis_size("ctx")
    seqs = lax.axis_size("dp")
    me_dp, me_ctx = lax.axis_index("dp"), lax.axis_index("ctx")
    blocks = input_scales.shape[2]
    chans = width // (ctx * seqs)
    share = tokens // seqs
    bf16 = jnp.bfloat16

    with jax.named_scope("gather_cotangent"):
        cotangent = lax.all_gather(out_grad[0], "dp", axis=0)
    with jax.named_scope("gather_weight"):
        weight = lax.all_gather(proj_weight, "ctx", axis=0, tiled=True)

    with jax.named_scope("signal"):
        signal = (
            (quant_input[0].reshape(tokens, blocks, width // blocks) * input_scales[0][:, :, None])
            .reshape(tokens, width)
            .astype(bf16)
        )
        parts = signal.T.reshape(seqs, ctx, chans, tokens)
        taps = lax.dynamic_slice_in_dim(filter_taps, me_dp * share, share, axis=1)
        taps = taps.reshape(seqs, ctx, chans * share // LANES, LANES)
        load = jnp.concatenate([parts, taps], axis=2).transpose(1, 0, 2, 3)
        load = load.reshape(ctx * seqs, -1, LANES)
    with jax.named_scope("signal_a2a"):
        load = lax.all_to_all(load, ("ctx", "dp"), 0, 0)
    with jax.named_scope("signal_in"):
        x = load[:, :chans].transpose(1, 0, 2)
        h = load[:, chans:].reshape(ctx, seqs, chans, share).transpose(2, 0, 1, 3)
        h = h.reshape(chans, ctx, LANES)
        first = (me_dp * ctx + me_ctx) * chans
        own_skip = lax.dynamic_slice_in_dim(skip, first, chans)
    with jax.named_scope("conv"):
        conv = conv_call(x, h, own_skip, seqs)
        conv = conv.reshape(chans, ctx, seqs, LANES).transpose(1, 0, 2, 3)
    with jax.named_scope("conv_a2a"):
        conv = lax.all_to_all(conv, "ctx", 0, 0)
    with jax.named_scope("dconv"):
        dconv = lax.dot_general(
            weight, cotangent, (((1,), (2,)), ((), ())), preferred_element_type=jnp.float32
        ).astype(bf16)
        dconv = dconv.reshape(ctx, chans, seqs, LANES)
    with jax.named_scope("dconv_a2a"):
        dconv = lax.all_to_all(dconv, "ctx", 0, 0)
        dconv = dconv.transpose(1, 0, 2, 3).reshape(chans, ctx * seqs, LANES)
    factor = 1.0 / math.sqrt(seqs * tokens * ctx)
    with jax.named_scope("grad_proj"):
        partial = lax.dot_general(
            conv.reshape(ctx * chans, seqs, LANES),
            cotangent,
            (((1, 2), (0, 1)), ((), ())),
            preferred_element_type=jnp.float32,
        ).astype(bf16)
    with jax.named_scope("grad_proj_a2a"):
        partial = lax.all_to_all(partial.reshape(ctx, chans, width), "ctx", 0, 0)
        grad_proj = jnp.sum(partial.astype(jnp.float32), axis=0) * factor
    with jax.named_scope("grads"):
        grad_in, grad_taps = grad_call(x, dconv, h, own_skip, seqs, factor)
    with jax.named_scope("grad_in_a2a"):
        grad_in = lax.all_to_all(grad_in.transpose(1, 0, 2), ("ctx", "dp"), 0, 0)
        grad_in = grad_in.reshape(ctx, seqs, chans, LANES).transpose(1, 0, 2, 3)
        grad_in = grad_in.reshape(width, LANES).T
    with jax.named_scope("grad_filter"):
        span = ctx * LANES // seqs
        pieces = grad_taps.astype(bf16).reshape(chans, seqs, span).transpose(1, 0, 2)
        got = []
        for k in range(seqs):
            pairs = [
                (d * ctx + c, (c % seqs + k) % seqs * ctx + (d * ctx + c) // seqs)
                for d in range(seqs)
                for c in range(ctx)
            ]
            piece = lax.dynamic_index_in_dim(pieces, (me_ctx + k) % seqs, 0, keepdims=False)
            got.append(lax.ppermute(piece, ("dp", "ctx"), pairs))
        got = jnp.stack(got)
        grad_filter = jnp.concatenate(
            [
                lax.dynamic_index_in_dim(got, (me_dp - m + seqs) % seqs, 0, keepdims=False)
                for m in range(seqs)
            ],
            axis=0,
        ).astype(jnp.float32)
    return (grad_in[None], grad_filter, grad_proj)


def solution(mesh):
    placed = (
        P("dp", "ctx", None),
        P("dp", "ctx", None),
        P("dp", "ctx", None),
        P(None, "ctx"),
        P(),
        P(("dp", "ctx"), None),
    )
    return jax.shard_map(
        on_device,
        mesh=mesh,
        in_specs=placed,
        out_specs=(P("dp", "ctx", None), P("ctx", "dp"), P(("dp", "ctx"), None)),
        check_vma=False,
    )
```

```python
import functools
import math

import jax
import jax.numpy as jnp
from jax import lax
from jax.experimental import pallas as pl
from jax.experimental.pallas import tpu as pltpu
from jax.sharding import Mesh, PartitionSpec as P

LANES = 128
HALF = LANES // 2
GROUP = 4
f32, bf16 = jnp.float32, jnp.bfloat16


def iota(rows, axis):
    return lax.broadcasted_iota(jnp.int32, (rows, LANES), axis)


def turn(field, by):
    return pltpu.roll(field, by, 1)


def moved(field, by):
    if by == 0:
        return field
    gap = jnp.zeros((abs(by), LANES), field.dtype)
    if by > 0:
        return jnp.concatenate([gap, field[:-by]], axis=0)
    return jnp.concatenate([field[-by:], gap], axis=0)


def mirror():
    return (iota(LANES, 0) + iota(LANES, 1) == LANES - 1).astype(bf16)


def tap_rows(taps, first, before):
    same = iota(HALF, 1) >= iota(HALF, 0)
    parts = []
    for delta in range(first, first + GROUP):
        line = jnp.broadcast_to(taps[delta : delta + 1, :], (HALF, LANES))
        here = pltpu.roll(line, 0, 1, stride=1, stride_axis=0)
        parts.append(jnp.where(same, here, before).astype(bf16))
        before = here
    return jnp.concatenate(parts, axis=0), before


def correlate(field, taps, seqs, sign):
    rows, span = field.shape[0], GROUP * seqs
    low = iota(rows, 1) < HALF
    beside = moved(field, sign * seqs)
    halves = [
        jnp.where(low, field, turn(beside, HALF)),
        jnp.where(low, turn(field, HALF), beside),
    ]
    wide = [
        jnp.concatenate([h.astype(bf16), moved(h, sign * 2 * seqs).astype(bf16)], axis=1)
        for h in halves
    ]
    total = [jnp.zeros((rows, LANES), f32)] * 2
    before = jnp.zeros((HALF, LANES), f32)
    for k in range(rows // span):
        matrix, before = tap_rows(taps, k * GROUP, before)
        cut = k * span
        kept = [w[: rows - cut] if sign > 0 else w[cut:] for w in wide]
        part = jnp.dot(jnp.concatenate(kept, axis=0), matrix, preferred_element_type=f32)
        for p in range(2):
            add = part[p * (rows - cut) : (p + 1) * (rows - cut)]
            if cut:
                gap = jnp.zeros((cut, LANES), f32)
                add = jnp.concatenate([gap, add] if sign > 0 else [add, gap], axis=0)
            total[p] = total[p] + add
    across = turn(total[1], HALF)
    return total[0] + jnp.where(low, moved(across, sign * seqs), across)


def conv_kernel(seqs, skip_ref, x_ref, h_ref, y_ref):
    x = x_ref[0].astype(f32)
    y = correlate(x, h_ref[0].astype(f32), seqs, 1)
    y_ref[0] = (y + x * skip_ref[pl.program_id(0)]).astype(bf16)


def back_kernel(seqs, skip_ref, d_ref, h_ref, y_ref):
    flip = mirror()
    d = jnp.dot(d_ref[0], flip, preferred_element_type=f32)
    y = correlate(d, h_ref[0].astype(f32), seqs, -1)
    y = (y + d * skip_ref[pl.program_id(0)]).astype(bf16)
    y_ref[0] = jnp.dot(y, flip, preferred_element_type=f32).astype(bf16)


def taps_kernel(seqs, scale, x_ref, d_ref, f_ref, long_ref):
    x, d = x_ref[0].astype(f32), d_ref[0].astype(f32)
    rows, span = x.shape[0], GROUP * seqs
    flip = mirror()
    left = []
    for v in range(GROUP):
        part = moved(x, v * seqs).astype(bf16)
        part = lax.dot_general(flip, part, (((1,), (1,)), ((), ())), preferred_element_type=f32)
        part = part.astype(bf16)
        left.append(jnp.concatenate([part[HALF:], part[:HALF]], axis=1))
    left = jnp.concatenate(left, axis=0)
    across = turn(d, HALF)
    shifted = jnp.where(iota(rows, 1) < HALF, across, moved(across, -seqs))
    for p, part in enumerate((d, shifted)):
        long_ref[p, :rows, :] = part.astype(bf16)
        long_ref[p, rows:, :] = jnp.zeros((rows, LANES), bf16)
    same = iota(HALF, 0) + iota(HALF, 1) >= HALF - 1
    after = jnp.zeros((HALF, LANES), f32)

    def outer(k):
        right = [
            jnp.concatenate(
                [long_ref[p, at * span : at * span + rows, :] for p in range(2)], axis=0
            )
            for at in (k, k + 1)
        ]
        return jnp.dot(left, jnp.concatenate(right, axis=1), preferred_element_type=f32)

    steps = list(reversed(range(0, rows // span, 2)))
    ready = outer(steps[0])
    for i, k in enumerate(steps):
        now = ready
        if i + 1 < len(steps):
            ready = outer(steps[i + 1])
        for j in reversed(range(2 * GROUP)):
            at, v = j // GROUP, j % GROUP
            here = now[v * HALF : (v + 1) * HALF, at * LANES : (at + 1) * LANES]
            lined = pltpu.roll(
                jnp.where(same, here, after), HALF + 1, 1, stride=1, stride_axis=0
            )
            delta = k * GROUP + j
            f_ref[0, delta : delta + 1, :] = jnp.sum(lined, axis=0, keepdims=True) * scale
            after = here


def per_channel(shape):
    return pl.BlockSpec((1, *shape[1:]), lambda i: (i, 0, 0))


def estimate(flops):
    return pl.CostEstimate(flops=flops, bytes_accessed=1 << 20, transcendentals=0)


def conv_call(kernel, field, taps, skip, seqs):
    chans, rows = taps.shape[0], field.shape[1]
    return pl.pallas_call(
        functools.partial(kernel, seqs),
        grid=(chans,),
        in_specs=[
            pl.BlockSpec(memory_space=pltpu.SMEM),
            per_channel(field.shape),
            per_channel(taps.shape),
        ],
        out_specs=per_channel(field.shape),
        out_shape=jax.ShapeDtypeStruct((chans, rows, LANES), bf16),
        compiler_params=pltpu.CompilerParams(vmem_limit_bytes=24 << 20),
        cost_estimate=estimate(5 << 30),
    )(skip, field, taps)


def taps_call(x, d, seqs, scale):
    chans, rows, _ = d.shape
    out = jax.ShapeDtypeStruct((chans, rows // seqs, LANES), f32)
    return pl.pallas_call(
        functools.partial(taps_kernel, seqs, scale),
        grid=(chans,),
        in_specs=[per_channel(x.shape)] * 2,
        out_specs=per_channel(out.shape),
        out_shape=out,
        scratch_shapes=[pltpu.VMEM((2, 2 * rows, LANES), bf16)],
        compiler_params=pltpu.CompilerParams(vmem_limit_bytes=24 << 20),
        cost_estimate=estimate(8 << 30),
    )(x, d)


def dconv_kernel(place_ref, w_ref, *refs):
    *pieces, out_ref = refs
    weight = w_ref[...]
    for j, piece in enumerate(pieces):
        part = lax.dot_general(
            weight, piece[...], (((1,), (1,)), ((), ())), preferred_element_type=jnp.float32
        )
        out_ref[:, pl.ds(place_ref[j], 1)] = (
            part.astype(jnp.bfloat16).reshape(out_ref.shape[0], 1, *out_ref.shape[2:])
        )


def proj_kernel(place_ref, c_ref, *refs):
    *pieces, out_ref, lhs_ref = refs
    rows, width = out_ref.shape
    for j in range(len(pieces)):
        part = c_ref[:, pl.ds(place_ref[j], 1)]
        lhs_ref[:, j * LANES : (j + 1) * LANES] = part.reshape(rows, LANES)
    step = 512
    for at in range(0, width, step):
        total = jnp.zeros((rows, step), jnp.float32)
        for j, piece in enumerate(pieces):
            total += jnp.dot(
                lhs_ref[:, j * LANES : (j + 1) * LANES],
                piece[:, at : at + step],
                preferred_element_type=jnp.float32,
            )
        out_ref[:, at : at + step] = total.astype(jnp.bfloat16)


def whole(count):
    return [pl.BlockSpec(memory_space=pltpu.VMEM)] * count


def dconv_call(place, weight, pieces, plane):
    rows = weight.shape[0]
    return pl.pallas_call(
        dconv_kernel,
        in_specs=[pl.BlockSpec(memory_space=pltpu.SMEM), *whole(1 + len(pieces))],
        out_specs=whole(1)[0],
        out_shape=jax.ShapeDtypeStruct((plane, len(pieces), rows // plane, LANES), jnp.bfloat16),
        compiler_params=pltpu.CompilerParams(vmem_limit_bytes=32 << 20),
        cost_estimate=pl.CostEstimate(flops=1 << 30, bytes_accessed=6 << 20, transcendentals=0),
    )(place, weight, *pieces)


def proj_call(place, conv, pieces):
    rows = conv.shape[0] * conv.shape[2]
    width = pieces[0].shape[1]
    return pl.pallas_call(
        proj_kernel,
        in_specs=[pl.BlockSpec(memory_space=pltpu.SMEM), *whole(1 + len(pieces))],
        out_specs=whole(1)[0],
        out_shape=jax.ShapeDtypeStruct((rows, width), jnp.bfloat16),
        scratch_shapes=[pltpu.VMEM((rows, len(pieces) * LANES), jnp.bfloat16)],
        compiler_params=pltpu.CompilerParams(vmem_limit_bytes=32 << 20),
        cost_estimate=pl.CostEstimate(flops=1 << 30, bytes_accessed=6 << 20, transcendentals=0),
    )(place, conv, *pieces)


SEQ = ("zl", "core")
POS = ("zh", "y", "x")
PLANE = ("y", "x")
COLUMN = ("zl", "core", "zh")


def column_pairs(step, other):
    pairs = []
    for z in range(4):
        for core in range(2):
            to, to_core = (z + step) % 4, core ^ other
            pairs.append(
                (z % 2 * 4 + core * 2 + z // 2, to % 2 * 4 + to_core * 2 + to // 2)
            )
    return pairs


def move(a, step, other=0):
    return lax.ppermute(a, COLUMN, column_pairs(step, other))


def places():
    z = 2 * lax.axis_index("zh") + lax.axis_index("zl")
    core = lax.axis_index("core")
    place = [(z + step) % 4 * 2 + (core + other) % 2 for other in (0, 1) for step in (0, 3, 1, 2)]
    return jnp.stack(place).astype(jnp.int32)


def on_device(quant_input, input_scales, out_grad, filter_taps, skip, proj_weight):
    tokens, width = quant_input.shape[1:]
    ctx, seqs, plane = (lax.axis_size(a) for a in (POS, SEQ, PLANE))
    me_dp, me_ctx = lax.axis_index(SEQ), lax.axis_index(POS)
    blocks = input_scales.shape[2]
    chans = width // (ctx * seqs)
    column = ctx * seqs // plane

    with jax.named_scope("share_cotangent"):
        own, place = out_grad[0], places()
        below, above, beside = move(own, 1), move(own, 3), move(own, 0, 1)
    with jax.named_scope("weight_a2a"):
        copies = jnp.broadcast_to(proj_weight[None], (plane, *proj_weight.shape))
        weight = lax.all_to_all(copies, PLANE, 0, 0).reshape(-1, width)
    with jax.named_scope("signal"):
        signal = (
            (quant_input[0].reshape(tokens, blocks, width // blocks) * input_scales[0][:, :, None])
            .reshape(tokens, width)
            .astype(bf16)
        )
        parts = signal.T.reshape(seqs, ctx, chans, tokens)
        taps = filter_taps.reshape(seqs, ctx, seqs, chans // seqs, tokens)
        taps = lax.dynamic_index_in_dim(taps, me_dp, 2, keepdims=False)
        load = jnp.concatenate([parts, taps], axis=2).transpose(1, 0, 2, 3)
        load = load.reshape(ctx * seqs, -1, LANES)
    with jax.named_scope("signal_a2a"):
        load, weight = lax.optimization_barrier((load, weight))
        load = lax.all_to_all(load, POS + SEQ, 0, 0)
    with jax.named_scope("share_far"):
        half = tokens // 2
        far = [move(below[:half], 1), move(above[half:], 3)]
        near = [move(a, 0, 1) for a in (below, above)]
        load, *far = lax.optimization_barrier((load, *far))
    with jax.named_scope("signal_in"):
        field = load.transpose(1, 0, 2)
        h = field[chans:].reshape(chans // seqs, ctx, seqs, LANES).transpose(2, 0, 1, 3)
        h = h.reshape(chans, ctx, LANES)
        first = (me_dp * ctx + me_ctx) * chans
        own_skip = lax.dynamic_slice_in_dim(skip, first, chans)
    with jax.named_scope("share_core"):
        far = jnp.concatenate(far, axis=0)
        pieces = [own, below, above, far, beside, *near, move(far, 0, 1)]
    with jax.named_scope("conv"):
        conv = conv_call(conv_kernel, field, h, own_skip, seqs)
        conv = conv.reshape(chans, ctx // plane, plane, seqs, LANES).transpose(2, 1, 3, 0, 4)
        conv = conv.reshape(plane, column, chans, LANES)
    with jax.named_scope("dconv"):
        dconv = dconv_call(place, weight, pieces, plane)
    with jax.named_scope("middle_a2a"):
        both = lax.all_to_all(jnp.concatenate([conv, dconv], axis=1), PLANE, 0, 0)
    with jax.named_scope("dconv_in"):
        dconv = both[:, column:].reshape(plane, ctx // plane, seqs, chans, LANES)
        dconv = dconv.transpose(3, 1, 0, 2, 4).reshape(chans, ctx * seqs, LANES)
    factor = 1.0 / math.sqrt(seqs * tokens * ctx)
    with jax.named_scope("grad_in"):
        grad_in = conv_call(back_kernel, dconv, h, own_skip, seqs).transpose(1, 0, 2)
        grad_in, conv, dconv = lax.optimization_barrier((grad_in, both[:, :column], dconv))
    with jax.named_scope("grad_in_a2a"):
        grad_in = lax.all_to_all(grad_in, POS + SEQ, 0, 0)
    with jax.named_scope("grad_taps"):
        grad_taps = taps_call(field, dconv, seqs, factor)
    with jax.named_scope("grad_proj"):
        conv, grad_taps = lax.optimization_barrier((conv, grad_taps))
        partial = proj_call(place, conv, pieces)
    with jax.named_scope("grad_proj_a2a"):
        partial, grad_in = lax.optimization_barrier((partial, grad_in))
        partial = lax.all_to_all(partial.reshape(plane, chans, width), PLANE, 0, 0)
        grad_proj = jnp.sum(partial.astype(jnp.float32), axis=0) * factor
    with jax.named_scope("grad_in_out"):
        grad_in = grad_in.reshape(ctx, seqs, chans, LANES).transpose(1, 0, 2, 3)
        grad_in = grad_in.reshape(width, LANES).T
    with jax.named_scope("grad_filter"):
        span = ctx * LANES // seqs
        rounded = grad_taps.astype(bf16).reshape(chans, seqs, span).transpose(1, 0, 2)
        got = []
        for k in range(seqs):
            pairs = [
                (d * ctx + c, (c % seqs + k) % seqs * ctx + (d * ctx + c) // seqs)
                for d in range(seqs)
                for c in range(ctx)
            ]
            piece = lax.dynamic_index_in_dim(rounded, (me_ctx + k) % seqs, 0, keepdims=False)
            got.append(lax.ppermute(piece, SEQ + POS, pairs))
        got = jnp.stack(got)
        grad_filter = jnp.concatenate(
            [
                lax.dynamic_index_in_dim(got, (me_dp - m + seqs) % seqs, 0, keepdims=False)
                for m in range(seqs)
            ],
            axis=0,
        ).astype(jnp.float32)
    return (grad_in[None], grad_filter, grad_proj)


def solution(mesh):
    mesh = Mesh(mesh.devices.reshape(2, 2, 2, 4, 4), SEQ + POS)
    placed = (
        P(SEQ, POS, None),
        P(SEQ, POS, None),
        P(SEQ, POS, None),
        P(None, POS),
        P(),
        P(SEQ + POS, None),
    )
    return jax.shard_map(
        on_device,
        mesh=mesh,
        in_specs=placed,
        out_specs=(P(SEQ, POS, None), P(POS, SEQ), P(SEQ + POS, None)),
        check_vma=False,
    )
```

```python
import functools
import math

import jax
import jax.numpy as jnp
from jax import lax
from jax.experimental import pallas as pl
from jax.experimental.pallas import tpu as pltpu
from jax.sharding import Mesh, PartitionSpec as P

LANES = 128
HALF = LANES // 2
GROUP = 4
f32, bf16 = jnp.float32, jnp.bfloat16


def iota(rows, axis):
    return lax.broadcasted_iota(jnp.int32, (rows, LANES), axis)


def turn(field, by):
    return pltpu.roll(field, by, 1)


def moved(field, by):
    if by == 0:
        return field
    gap = jnp.zeros((abs(by), LANES), field.dtype)
    if by > 0:
        return jnp.concatenate([gap, field[:-by]], axis=0)
    return jnp.concatenate([field[-by:], gap], axis=0)


def mirror():
    return (iota(LANES, 0) + iota(LANES, 1) == LANES - 1).astype(bf16)


def tap_rows(taps, first, before):
    same = iota(HALF, 1) >= iota(HALF, 0)
    parts = []
    for delta in range(first, first + GROUP):
        line = jnp.broadcast_to(taps[delta : delta + 1, :], (HALF, LANES))
        here = pltpu.roll(line, 0, 1, stride=1, stride_axis=0)
        parts.append(jnp.where(same, here, before).astype(bf16))
        before = here
    return jnp.concatenate(parts, axis=0), before


def correlate(field, taps, seqs, sign):
    rows, span = field.shape[0], GROUP * seqs
    low = iota(rows, 1) < HALF
    beside = moved(field, sign * seqs)
    halves = [
        jnp.where(low, field, turn(beside, HALF)),
        jnp.where(low, turn(field, HALF), beside),
    ]
    wide = [
        jnp.concatenate([h.astype(bf16), moved(h, sign * 2 * seqs).astype(bf16)], axis=1)
        for h in halves
    ]
    total = [jnp.zeros((rows, LANES), f32)] * 2
    before = jnp.zeros((HALF, LANES), f32)
    for k in range(rows // span):
        matrix, before = tap_rows(taps, k * GROUP, before)
        cut = k * span
        kept = [w[: rows - cut] if sign > 0 else w[cut:] for w in wide]
        part = jnp.dot(jnp.concatenate(kept, axis=0), matrix, preferred_element_type=f32)
        for p in range(2):
            add = part[p * (rows - cut) : (p + 1) * (rows - cut)]
            if cut:
                gap = jnp.zeros((cut, LANES), f32)
                add = jnp.concatenate([gap, add] if sign > 0 else [add, gap], axis=0)
            total[p] = total[p] + add
    across = turn(total[1], HALF)
    return total[0] + jnp.where(low, moved(across, sign * seqs), across)


def conv_kernel(seqs, skip_ref, x_ref, h_ref, y_ref):
    many = x_ref.shape[0]
    for i in range(many):
        x = x_ref[i].astype(f32)
        y = correlate(x, h_ref[i].astype(f32), seqs, 1)
        y_ref[i] = (y + x * skip_ref[pl.program_id(0) * many + i]).astype(bf16)


def back_kernel(seqs, skip_ref, d_ref, h_ref, y_ref):
    many = d_ref.shape[0]
    for i in range(many):
        d = d_ref[i].astype(f32)
        y = correlate(d, h_ref[i].astype(f32), seqs, -1)
        y_ref[i] = (y + d * skip_ref[pl.program_id(0) * many + i]).astype(bf16)


def taps_kernel(seqs, scale_ref, x_ref, d_ref, f_ref, long_ref, sum_ref):
    many, rows, _ = x_ref.shape
    blocks, span = rows // seqs, GROUP * seqs
    same = (iota(LANES, 0) == iota(LANES, 1)).astype(bf16)
    keep = iota(HALF, 0) + iota(HALF, 1) < LANES
    step = pl.program_id(0)
    for i in range(many):
        x, d = x_ref[i].astype(f32), d_ref[i].astype(f32)
        left = []
        for v in range(GROUP):
            part = moved(x, v * seqs).astype(bf16)
            part = lax.dot_general(
                same, part, (((1,), (1,)), ((), ())), preferred_element_type=f32
            ).astype(bf16)
            left.append(jnp.concatenate([part[:HALF], part[HALF:]], axis=1))
        left = jnp.concatenate(left, axis=0)
        across = turn(d, HALF)
        shifted = jnp.where(iota(rows, 1) < HALF, moved(across, -seqs), across)
        for p, part in enumerate((d, shifted)):
            long_ref[i, p, :rows, :] = part.astype(bf16)
            long_ref[i, p, rows:, :] = jnp.zeros((rows, LANES), bf16)
        after = jnp.zeros((HALF, LANES), f32)

        def outer(k):
            right = [
                jnp.concatenate(
                    [long_ref[i, p, at * span : at * span + rows, :] for p in range(2)], axis=0
                )
                for at in (k, k + 1)
            ]
            return jnp.dot(left, jnp.concatenate(right, axis=1), preferred_element_type=f32)

        steps = list(reversed(range(0, rows // span, 2)))
        ready = outer(steps[0])
        for n, k in enumerate(steps):
            now = ready
            if n + 1 < len(steps):
                ready = outer(steps[n + 1])
            for j in reversed(range(2 * GROUP)):
                at, v = j // GROUP, j % GROUP
                here = now[v * HALF : (v + 1) * HALF, at * LANES : (at + 1) * LANES]
                lined = pltpu.roll(jnp.where(keep, here, after), 0, 1, stride=1, stride_axis=0)
                delta = k * GROUP + j
                sum_ref[pl.ds((step * many + i) * blocks + delta, 1), :] = (
                    jnp.sum(lined, axis=0, keepdims=True) * scale_ref[0]
                )
                after = here

    @pl.when(step == pl.num_programs(0) - 1)
    def _():
        f_ref[...] = jnp.dot(
            sum_ref[...].astype(bf16), mirror(), preferred_element_type=f32
        ).astype(bf16)


MANY = 4


def per_channel(many, shape):
    return pl.BlockSpec((many, *shape[1:]), lambda i: (i, 0, 0))


def estimate(flops):
    return pl.CostEstimate(flops=flops, bytes_accessed=1 << 16, transcendentals=0)


def conv_call(kernel, field, taps, skip, seqs):
    chans, rows = taps.shape[0], field.shape[1]
    return pl.pallas_call(
        functools.partial(kernel, seqs),
        grid=(chans // MANY,),
        in_specs=[
            pl.BlockSpec(memory_space=pltpu.SMEM),
            per_channel(MANY, field.shape),
            per_channel(MANY, taps.shape),
        ],
        out_specs=per_channel(MANY, field.shape),
        out_shape=jax.ShapeDtypeStruct((chans, rows, LANES), bf16),
        compiler_params=pltpu.CompilerParams(vmem_limit_bytes=24 << 20),
        cost_estimate=estimate(1 << 20),
    )(skip, field, taps)


def taps_call(x, d, seqs, scale):
    chans, rows, _ = d.shape
    out = jax.ShapeDtypeStruct((chans * rows // seqs, LANES), bf16)
    return pl.pallas_call(
        functools.partial(taps_kernel, seqs),
        grid=(chans // MANY,),
        in_specs=[
            pl.BlockSpec(memory_space=pltpu.SMEM),
            per_channel(MANY, x.shape),
            per_channel(MANY, d.shape),
        ],
        out_specs=pl.BlockSpec(out.shape, lambda i: (0, 0)),
        out_shape=out,
        scratch_shapes=[
            pltpu.VMEM((MANY, 2, 2 * rows, LANES), bf16),
            pltpu.VMEM(out.shape, f32),
        ],
        compiler_params=pltpu.CompilerParams(vmem_limit_bytes=24 << 20),
        cost_estimate=estimate(1 << 20),
    )(scale, x, d).reshape(chans, rows // seqs, LANES)


def dconv_kernel(place_ref, w_ref, *refs):
    *pieces, out_ref, weight_ref = refs
    for k in range(weight_ref.shape[1] // LANES):
        weight_ref[:, k * LANES : (k + 1) * LANES] = w_ref[:, k].reshape(-1, LANES)
    flip = mirror()
    for first in range(0, len(pieces), GROUP):
        block = jnp.concatenate([piece[...] for piece in pieces[first : first + GROUP]], axis=0)
        wide = lax.dot_general(
            weight_ref[...], block, (((1,), (1,)), ((), ())), preferred_element_type=f32
        ).astype(bf16)
        for j in range(GROUP):
            part = wide[:, j * LANES : (j + 1) * LANES]
            part = jnp.dot(part, flip, preferred_element_type=f32).astype(bf16)
            out_ref[:, pl.ds(place_ref[first + j], 1)] = part.reshape(
                out_ref.shape[0], 1, *out_ref.shape[2:]
            )


def proj_kernel(place_ref, c_ref, *refs):
    *pieces, out_ref, lhs_ref = refs
    rows, width = out_ref.shape
    ahead = c_ref.shape[1] - len(pieces)
    for j in range(len(pieces)):
        part = c_ref[:, pl.ds(ahead + place_ref[j], 1)]
        lhs_ref[:, j * LANES : (j + 1) * LANES] = part.reshape(rows, LANES)
    step = 512
    for at in range(0, width, step):
        block = jnp.concatenate([piece[:, at : at + step] for piece in pieces], axis=0)
        out_ref[:, at : at + step] = jnp.dot(
            lhs_ref[...], block, preferred_element_type=f32
        ).astype(bf16)


def whole(count):
    return [pl.BlockSpec(memory_space=pltpu.VMEM)] * count


def dconv_call(place, load, pieces):
    plane, _, chans, _ = load.shape
    return pl.pallas_call(
        dconv_kernel,
        in_specs=[pl.BlockSpec(memory_space=pltpu.SMEM), *whole(1 + len(pieces))],
        out_specs=whole(1)[0],
        out_shape=jax.ShapeDtypeStruct((plane, len(pieces), chans, LANES), bf16),
        scratch_shapes=[pltpu.VMEM((plane * chans, pieces[0].shape[1]), bf16)],
        compiler_params=pltpu.CompilerParams(vmem_limit_bytes=32 << 20),
        cost_estimate=pl.CostEstimate(flops=1 << 30, bytes_accessed=6 << 20, transcendentals=0),
    )(place, load, *pieces)


def proj_call(place, conv, pieces):
    rows = conv.shape[0] * conv.shape[2]
    width = pieces[0].shape[1]
    return pl.pallas_call(
        proj_kernel,
        in_specs=[pl.BlockSpec(memory_space=pltpu.SMEM), *whole(1 + len(pieces))],
        out_specs=whole(1)[0],
        out_shape=jax.ShapeDtypeStruct((rows, width), jnp.bfloat16),
        scratch_shapes=[pltpu.VMEM((rows, len(pieces) * LANES), jnp.bfloat16)],
        compiler_params=pltpu.CompilerParams(vmem_limit_bytes=32 << 20),
        cost_estimate=pl.CostEstimate(flops=1 << 30, bytes_accessed=6 << 20, transcendentals=0),
    )(place, conv, *pieces)


SEQ = ("zl", "core")
POS = ("zh", "y", "x")
PLANE = ("y", "x")
COLUMN = ("zl", "core", "zh")


def column_pairs(step, other):
    pairs = []
    for z in range(4):
        for core in range(2):
            to, to_core = (z + step) % 4, core ^ other
            pairs.append(
                (z % 2 * 4 + core * 2 + z // 2, to % 2 * 4 + to_core * 2 + to // 2)
            )
    return pairs


def move(a, step, other=0):
    return lax.ppermute(a, COLUMN, column_pairs(step, other))


def places():
    z = 2 * lax.axis_index("zh") + lax.axis_index("zl")
    core = lax.axis_index("core")
    place = [(z + step) % 4 * 2 + (core + other) % 2 for other in (0, 1) for step in (0, 3, 1, 2)]
    return jnp.stack(place).astype(jnp.int32)


def on_device(quant_input, input_scales, out_grad, filter_taps, skip, proj_weight):
    tokens, width = quant_input.shape[1:]
    ctx, seqs, plane = (lax.axis_size(a) for a in (POS, SEQ, PLANE))
    me_dp, me_ctx = lax.axis_index(SEQ), lax.axis_index(POS)
    blocks = input_scales.shape[2]
    chans = width // (ctx * seqs)
    column = ctx * seqs // plane

    with jax.named_scope("signal"):
        signal = (
            (quant_input[0].reshape(tokens, blocks, width // blocks) * input_scales[0][:, :, None])
            .reshape(tokens, width)
            .astype(bf16)
        )
        parts = signal.T.reshape(seqs, ctx, chans, tokens)
        taps = filter_taps.reshape(seqs, ctx, seqs, chans // seqs, tokens)
        taps = lax.dynamic_index_in_dim(taps, me_dp, 2, keepdims=False)
        load = jnp.concatenate([parts, taps], axis=2).transpose(1, 0, 2, 3)
        load = load.reshape(ctx * seqs, -1, LANES)
    with jax.named_scope("signal_a2a"):
        load = lax.all_to_all(load, POS + SEQ, 0, 0)
    with jax.named_scope("signal_in"):
        x = load[:, :chans].transpose(1, 0, 2)
        h = load[:, chans:].reshape(ctx, seqs, chans // seqs, LANES).transpose(1, 2, 0, 3)
        h = h.reshape(chans, ctx, LANES)
        first = (me_dp * ctx + me_ctx) * chans
        own_skip = lax.dynamic_slice_in_dim(skip, first, chans)
    with jax.named_scope("share_cotangent"):
        own, h = lax.optimization_barrier((out_grad[0], h))
        place = places()
        below, above, beside = move(own, 1), move(own, 3), move(own, 0, 1)
        half = tokens // 2
        far = jnp.concatenate([move(below[:half], 1), move(above[half:], 3)], axis=0)
        pieces = [own, below, above, far, beside]
        pieces += [move(a, 0, 1) for a in (below, above, far)]
    with jax.named_scope("conv"):
        conv = conv_call(conv_kernel, x, h, own_skip, seqs)
        conv = conv.reshape(chans, ctx // plane, plane, seqs, LANES).transpose(2, 1, 3, 0, 4)
        conv = conv.reshape(plane, column, chans, LANES)
    with jax.named_scope("conv_a2a"):
        rows = proj_weight.reshape(chans, width // LANES, LANES).transpose(1, 0, 2)
        rows = jnp.broadcast_to(rows[None], (plane, *rows.shape))
        load = lax.all_to_all(jnp.concatenate([rows, conv], axis=1), PLANE, 0, 0)
    with jax.named_scope("dconv"):
        dconv = dconv_call(place, load, pieces)
    with jax.named_scope("dconv_a2a"):
        dconv = lax.all_to_all(dconv, PLANE, 0, 0)
        dconv = dconv.reshape(plane, ctx // plane, seqs, chans, LANES)
        dconv = dconv.transpose(3, 1, 0, 2, 4).reshape(chans, ctx * seqs, LANES)
    factor = 1.0 / math.sqrt(seqs * tokens * ctx)
    with jax.named_scope("grad_proj"):
        partial = proj_call(place, load, pieces)
        partial, scale, own_skip = lax.optimization_barrier(
            (partial, jnp.full((1,), factor, f32), own_skip)
        )
    with jax.named_scope("grad_taps"):
        grad_taps = taps_call(x, dconv, seqs, scale)
        pairs = []
        for d in range(seqs):
            for c in range(ctx):
                at, x_row = (d * ctx + c) // seqs, c % seqs
                pairs.append((d * ctx + c, x_row * ctx + at))
        held = lax.ppermute(grad_taps, SEQ + POS, pairs)
    with jax.named_scope("grad_in"):
        grad_in = conv_call(back_kernel, dconv, h, own_skip, seqs).transpose(1, 0, 2)
    with jax.named_scope("grad_proj_a2a"):
        partial = lax.all_to_all(partial.reshape(plane, chans, width), PLANE, 0, 0)
        partial, held = lax.optimization_barrier((partial, held))
        grad_proj = jnp.sum(partial.astype(f32), axis=0) * factor
    with jax.named_scope("grad_in_a2a"):
        grad_in = lax.all_to_all(grad_in, POS + SEQ, 0, 0)
    with jax.named_scope("grad_in_out"):
        grad_in = grad_in.reshape(ctx, seqs, chans, LANES).transpose(1, 0, 2, 3)
        grad_in = lax.dot_general(
            mirror(), grad_in.reshape(width, LANES), (((1,), (1,)), ((), ())),
            preferred_element_type=f32,
        ).astype(bf16)
    with jax.named_scope("grad_filter"):
        held = held.reshape(chans, seqs, ctx // seqs, LANES).transpose(1, 0, 2, 3)
        got = []
        for k in range(seqs):
            piece = lax.dynamic_index_in_dim(held, me_dp ^ k, 0, keepdims=False)
            if k:
                piece = lax.ppermute(piece, SEQ, [(i, i ^ k) for i in range(seqs)])
            got.append(piece)
        got = jnp.stack(got)
        grad_filter = jnp.concatenate(
            [lax.dynamic_index_in_dim(got, me_dp ^ m, 0, keepdims=False) for m in range(seqs)],
            axis=0,
        )
        grad_filter = grad_filter.reshape(seqs * chans, -1).astype(f32)
    return (grad_in[None], grad_filter, grad_proj)


def solution(mesh):
    mesh = Mesh(mesh.devices.reshape(2, 2, 2, 4, 4), SEQ + POS)
    placed = (
        P(SEQ, POS, None),
        P(SEQ, POS, None),
        P(SEQ, POS, None),
        P(None, POS),
        P(),
        P(SEQ + POS, None),
    )
    return jax.shard_map(
        on_device,
        mesh=mesh,
        in_specs=placed,
        out_specs=(P(SEQ, POS, None), P(POS, SEQ), P(SEQ + POS, None)),
        check_vma=False,
    )
```

```python
import functools
import math

import jax
import jax.numpy as jnp
from jax import lax
from jax.experimental import pallas as pl
from jax.experimental.pallas import tpu as pltpu
from jax.sharding import Mesh, PartitionSpec as P

LANES = 128
HALF = LANES // 2
GROUP = 4
f32, bf16 = jnp.float32, jnp.bfloat16


def iota(rows, axis):
    return lax.broadcasted_iota(jnp.int32, (rows, LANES), axis)


def turn(field, by):
    return pltpu.roll(field, by, 1)


def moved(field, by):
    if by == 0:
        return field
    gap = jnp.zeros((abs(by), LANES), field.dtype)
    if by > 0:
        return jnp.concatenate([gap, field[:-by]], axis=0)
    return jnp.concatenate([field[-by:], gap], axis=0)


def mirror():
    return (iota(LANES, 0) + iota(LANES, 1) == LANES - 1).astype(bf16)


def tap_rows(taps, first, before):
    same = iota(HALF, 1) >= iota(HALF, 0)
    parts = []
    for delta in range(first, first + GROUP):
        line = jnp.broadcast_to(taps[delta : delta + 1, :], (HALF, LANES))
        here = pltpu.roll(line, 0, 1, stride=1, stride_axis=0)
        parts.append(jnp.where(same, here, before).astype(bf16))
        before = here
    return jnp.concatenate(parts, axis=0), before


def correlate(field, taps, seqs, sign):
    rows, span = field.shape[0], GROUP * seqs
    low = iota(rows, 1) < HALF
    beside = moved(field, sign * seqs)
    halves = [
        jnp.where(low, field, turn(beside, HALF)),
        jnp.where(low, turn(field, HALF), beside),
    ]
    wide = [
        jnp.concatenate([h.astype(bf16), moved(h, sign * 2 * seqs).astype(bf16)], axis=1)
        for h in halves
    ]
    total = [jnp.zeros((rows, LANES), f32)] * 2
    before = jnp.zeros((HALF, LANES), f32)
    for k in range(rows // span):
        matrix, before = tap_rows(taps, k * GROUP, before)
        cut = k * span
        kept = [w[: rows - cut] if sign > 0 else w[cut:] for w in wide]
        part = jnp.dot(jnp.concatenate(kept, axis=0), matrix, preferred_element_type=f32)
        for p in range(2):
            add = part[p * (rows - cut) : (p + 1) * (rows - cut)]
            if cut:
                gap = jnp.zeros((cut, LANES), f32)
                add = jnp.concatenate([gap, add] if sign > 0 else [add, gap], axis=0)
            total[p] = total[p] + add
    across = turn(total[1], HALF)
    return total[0] + jnp.where(low, moved(across, sign * seqs), across)


def conv_kernel(seqs, skip_ref, x_ref, h_ref, y_ref):
    many = x_ref.shape[0]
    for i in range(many):
        x = x_ref[i].astype(f32)
        y = correlate(x, h_ref[i].astype(f32), seqs, 1)
        y_ref[i] = (y + x * skip_ref[pl.program_id(0) * many + i]).astype(bf16)


def back_kernel(seqs, skip_ref, d_ref, h_ref, y_ref):
    many = d_ref.shape[0]
    for i in range(many):
        d = d_ref[i].astype(f32)
        y = correlate(d, h_ref[i].astype(f32), seqs, -1)
        y_ref[i] = (y + d * skip_ref[pl.program_id(0) * many + i]).astype(bf16)


def taps_kernel(seqs, scale_ref, x_ref, d_ref, f_ref, long_ref, sum_ref):
    many, rows, _ = x_ref.shape
    blocks, span = rows // seqs, GROUP * seqs
    same = (iota(LANES, 0) == iota(LANES, 1)).astype(bf16)
    keep = iota(HALF, 0) + iota(HALF, 1) < LANES
    step = pl.program_id(0)
    for i in range(many):
        x, d = x_ref[i].astype(f32), d_ref[i].astype(f32)
        left = []
        for v in range(GROUP):
            part = moved(x, v * seqs).astype(bf16)
            part = lax.dot_general(
                same, part, (((1,), (1,)), ((), ())), preferred_element_type=f32
            ).astype(bf16)
            left.append(jnp.concatenate([part[:HALF], part[HALF:]], axis=1))
        left = jnp.concatenate(left, axis=0)
        across = turn(d, HALF)
        shifted = jnp.where(iota(rows, 1) < HALF, moved(across, -seqs), across)
        for p, part in enumerate((d, shifted)):
            long_ref[i, p, :rows, :] = part.astype(bf16)
            long_ref[i, p, rows:, :] = jnp.zeros((rows, LANES), bf16)
        after = jnp.zeros((HALF, LANES), f32)

        def outer(k):
            right = [
                jnp.concatenate(
                    [long_ref[i, p, at * span : at * span + rows, :] for p in range(2)], axis=0
                )
                for at in (k, k + 1)
            ]
            return jnp.dot(left, jnp.concatenate(right, axis=1), preferred_element_type=f32)

        steps = list(reversed(range(0, rows // span, 2)))
        ready = outer(steps[0])
        for n, k in enumerate(steps):
            now = ready
            if n + 1 < len(steps):
                ready = outer(steps[n + 1])
            for j in reversed(range(2 * GROUP)):
                at, v = j // GROUP, j % GROUP
                here = now[v * HALF : (v + 1) * HALF, at * LANES : (at + 1) * LANES]
                lined = pltpu.roll(jnp.where(keep, here, after), 0, 1, stride=1, stride_axis=0)
                delta = k * GROUP + j
                sum_ref[pl.ds((step * many + i) * blocks + delta, 1), :] = (
                    jnp.sum(lined, axis=0, keepdims=True) * scale_ref[0]
                )
                after = here

    @pl.when(step == pl.num_programs(0) - 1)
    def _():
        f_ref[...] = jnp.dot(
            sum_ref[...].astype(bf16), mirror(), preferred_element_type=f32
        ).astype(bf16)


MANY = 4


def per_channel(many, shape):
    return pl.BlockSpec((many, *shape[1:]), lambda i: (i, 0, 0))


def estimate(flops):
    return pl.CostEstimate(flops=flops, bytes_accessed=1 << 16, transcendentals=0)


def conv_call(kernel, field, taps, skip, seqs):
    chans, rows = taps.shape[0], field.shape[1]
    return pl.pallas_call(
        functools.partial(kernel, seqs),
        grid=(chans // MANY,),
        in_specs=[
            pl.BlockSpec(memory_space=pltpu.SMEM),
            per_channel(MANY, field.shape),
            per_channel(MANY, taps.shape),
        ],
        out_specs=per_channel(MANY, field.shape),
        out_shape=jax.ShapeDtypeStruct((chans, rows, LANES), bf16),
        compiler_params=pltpu.CompilerParams(vmem_limit_bytes=24 << 20),
        cost_estimate=estimate(1 << 20),
    )(skip, field, taps)


def taps_call(x, d, seqs, scale):
    chans, rows, _ = d.shape
    out = jax.ShapeDtypeStruct((chans * rows // seqs, LANES), bf16)
    return pl.pallas_call(
        functools.partial(taps_kernel, seqs),
        grid=(chans // MANY,),
        in_specs=[
            pl.BlockSpec(memory_space=pltpu.SMEM),
            per_channel(MANY, x.shape),
            per_channel(MANY, d.shape),
        ],
        out_specs=pl.BlockSpec(out.shape, lambda i: (0, 0)),
        out_shape=out,
        scratch_shapes=[
            pltpu.VMEM((MANY, 2, 2 * rows, LANES), bf16),
            pltpu.VMEM(out.shape, f32),
        ],
        compiler_params=pltpu.CompilerParams(vmem_limit_bytes=24 << 20),
        cost_estimate=estimate(1 << 20),
    )(scale, x, d).reshape(chans, rows // seqs, LANES)


def dconv_kernel(place_ref, w_ref, *refs):
    *pieces, out_ref, weight_ref = refs
    for k in range(weight_ref.shape[1] // LANES):
        weight_ref[:, k * LANES : (k + 1) * LANES] = w_ref[:, k].reshape(-1, LANES)
    flip = mirror()
    for first in range(0, len(pieces), GROUP):
        block = jnp.concatenate([piece[...] for piece in pieces[first : first + GROUP]], axis=0)
        wide = lax.dot_general(
            weight_ref[...], block, (((1,), (1,)), ((), ())), preferred_element_type=f32
        ).astype(bf16)
        for j in range(GROUP):
            part = wide[:, j * LANES : (j + 1) * LANES]
            part = jnp.dot(part, flip, preferred_element_type=f32).astype(bf16)
            out_ref[:, pl.ds(place_ref[first + j], 1)] = part.reshape(
                out_ref.shape[0], 1, *out_ref.shape[2:]
            )


def proj_kernel(place_ref, c_ref, *refs):
    *pieces, out_ref, lhs_ref = refs
    rows, width = out_ref.shape
    ahead = c_ref.shape[1] - len(pieces)
    for j in range(len(pieces)):
        part = c_ref[:, pl.ds(ahead + place_ref[j], 1)]
        lhs_ref[:, j * LANES : (j + 1) * LANES] = part.reshape(rows, LANES)
    step = 512
    for at in range(0, width, step):
        block = jnp.concatenate([piece[:, at : at + step] for piece in pieces], axis=0)
        out_ref[:, at : at + step] = jnp.dot(
            lhs_ref[...], block, preferred_element_type=f32
        ).astype(bf16)


def whole(count):
    return [pl.BlockSpec(memory_space=pltpu.VMEM)] * count


def dconv_call(place, load, pieces):
    plane, _, chans, _ = load.shape
    return pl.pallas_call(
        dconv_kernel,
        in_specs=[pl.BlockSpec(memory_space=pltpu.SMEM), *whole(1 + len(pieces))],
        out_specs=whole(1)[0],
        out_shape=jax.ShapeDtypeStruct((plane, len(pieces), chans, LANES), bf16),
        scratch_shapes=[pltpu.VMEM((plane * chans, pieces[0].shape[1]), bf16)],
        compiler_params=pltpu.CompilerParams(vmem_limit_bytes=32 << 20),
        cost_estimate=pl.CostEstimate(flops=1 << 30, bytes_accessed=6 << 20, transcendentals=0),
    )(place, load, *pieces)


def proj_call(place, conv, pieces):
    rows = conv.shape[0] * conv.shape[2]
    width = pieces[0].shape[1]
    return pl.pallas_call(
        proj_kernel,
        in_specs=[pl.BlockSpec(memory_space=pltpu.SMEM), *whole(1 + len(pieces))],
        out_specs=whole(1)[0],
        out_shape=jax.ShapeDtypeStruct((rows, width), jnp.bfloat16),
        scratch_shapes=[pltpu.VMEM((rows, len(pieces) * LANES), jnp.bfloat16)],
        compiler_params=pltpu.CompilerParams(vmem_limit_bytes=32 << 20),
        cost_estimate=pl.CostEstimate(flops=1 << 30, bytes_accessed=6 << 20, transcendentals=0),
    )(place, conv, *pieces)


SEQ = ("zl", "core")
POS = ("zh", "y", "x")
PLANE = ("y", "x")
COLUMN = ("zl", "core", "zh")


def column_pairs(step, other):
    pairs = []
    for z in range(4):
        for core in range(2):
            to, to_core = (z + step) % 4, core ^ other
            pairs.append(
                (z % 2 * 4 + core * 2 + z // 2, to % 2 * 4 + to_core * 2 + to // 2)
            )
    return pairs


def move(a, step, other=0):
    return lax.ppermute(a, COLUMN, column_pairs(step, other))


def places():
    z = 2 * lax.axis_index("zh") + lax.axis_index("zl")
    core = lax.axis_index("core")
    place = [(z + step) % 4 * 2 + (core + other) % 2 for other in (0, 1) for step in (0, 3, 1, 2)]
    return jnp.stack(place).astype(jnp.int32)


def on_device(quant_input, input_scales, out_grad, filter_taps, skip, proj_weight):
    tokens, width = quant_input.shape[1:]
    ctx, seqs, plane = (lax.axis_size(a) for a in (POS, SEQ, PLANE))
    me_dp, me_ctx = lax.axis_index(SEQ), lax.axis_index(POS)
    blocks = input_scales.shape[2]
    chans = width // (ctx * seqs)
    column = ctx * seqs // plane

    with jax.named_scope("signal"):
        signal = (
            (quant_input[0].reshape(tokens, blocks, width // blocks) * input_scales[0][:, :, None])
            .reshape(tokens, width)
            .astype(bf16)
        )
        parts = signal.T.reshape(seqs, ctx, chans, tokens)
        taps = filter_taps.reshape(seqs, ctx, seqs, chans // seqs, tokens)
        taps = lax.dynamic_index_in_dim(taps, me_dp, 2, keepdims=False)
        load = jnp.concatenate([parts, taps], axis=2).transpose(1, 0, 2, 3)
        load = load.reshape(ctx * seqs, -1, chans // seqs, LANES)
    with jax.named_scope("signal_a2a"):
        load = lax.all_to_all(load, POS + SEQ, 0, 0)
        load = load.reshape(ctx * seqs, -1, LANES)
    with jax.named_scope("signal_in"):
        x = load[:, :chans].transpose(1, 0, 2)
        h = load[:, chans:].reshape(ctx, seqs, chans // seqs, LANES).transpose(1, 2, 0, 3)
        h = h.reshape(chans, ctx, LANES)
        first = (me_dp * ctx + me_ctx) * chans
        own_skip = lax.dynamic_slice_in_dim(skip, first, chans)
    with jax.named_scope("share_cotangent"):
        own = out_grad[0]
        place = places()
        below, above, beside = move(own, 1), move(own, 3), move(own, 0, 1)
        half = tokens // 2
        far = jnp.concatenate([move(below[:half], 1), move(above[half:], 3)], axis=0)
        pieces = [own, below, above, far, beside]
        pieces += [move(a, 0, 1) for a in (below, above, far)]
    with jax.named_scope("conv"):
        conv = conv_call(conv_kernel, x, h, own_skip, seqs)
        conv = conv.reshape(chans, ctx // plane, plane, seqs, LANES).transpose(2, 1, 3, 0, 4)
        conv = conv.reshape(plane, column, chans, LANES)
    with jax.named_scope("conv_a2a"):
        rows = proj_weight.reshape(chans, width // LANES, LANES).transpose(1, 0, 2)
        rows = jnp.broadcast_to(rows[None], (plane, *rows.shape))
        load = lax.all_to_all(jnp.concatenate([rows, conv], axis=1), PLANE, 0, 0)
    with jax.named_scope("dconv"):
        dconv = dconv_call(place, load, pieces)
    with jax.named_scope("dconv_a2a"):
        dconv = lax.all_to_all(dconv, PLANE, 0, 0)
        dconv = dconv.reshape(plane, ctx // plane, seqs, chans, LANES)
        dconv = dconv.transpose(3, 1, 0, 2, 4).reshape(chans, ctx * seqs, LANES)
    factor = 1.0 / math.sqrt(seqs * tokens * ctx)
    with jax.named_scope("grad_proj"):
        partial = proj_call(place, load, pieces)
        partial, scale, own_skip = lax.optimization_barrier(
            (partial, jnp.full((1,), factor, f32), own_skip)
        )
    with jax.named_scope("grad_taps"):
        grad_taps = taps_call(x, dconv, seqs, scale)
        pairs = []
        for d in range(seqs):
            for c in range(ctx):
                at, x_row = (d * ctx + c) // seqs, c % seqs
                pairs.append((d * ctx + c, x_row * ctx + at))
        held = lax.ppermute(grad_taps, SEQ + POS, pairs)
    with jax.named_scope("grad_in"):
        grad_in = conv_call(back_kernel, dconv, h, own_skip, seqs).transpose(1, 0, 2)
    with jax.named_scope("grad_proj_a2a"):
        partial = lax.all_to_all(partial.reshape(plane, chans, width), PLANE, 0, 0)
        partial, held = lax.optimization_barrier((partial, held))
        grad_proj = jnp.sum(partial.astype(f32), axis=0) * factor
    with jax.named_scope("grad_in_a2a"):
        grad_in = lax.all_to_all(grad_in, POS + SEQ, 0, 0)
    with jax.named_scope("grad_filter"):
        held = held.reshape(chans, seqs, ctx // seqs, LANES).transpose(1, 0, 2, 3)
        got = []
        for k in range(seqs):
            piece = lax.dynamic_index_in_dim(held, me_dp ^ k, 0, keepdims=False)
            if k:
                piece = lax.ppermute(piece, SEQ, [(i, i ^ k) for i in range(seqs)])
            got.append(piece)
        got = jnp.stack(got)
        grad_filter = jnp.concatenate(
            [lax.dynamic_index_in_dim(got, me_dp ^ m, 0, keepdims=False) for m in range(seqs)],
            axis=0,
        )
        grad_filter = grad_filter.reshape(seqs * chans, -1).astype(f32)
        flip, grad_filter = lax.optimization_barrier((mirror(), grad_filter))
    with jax.named_scope("grad_in_out"):
        grad_in = grad_in.reshape(ctx, seqs, chans, LANES).transpose(1, 0, 2, 3)
        grad_in = lax.dot_general(
            flip, grad_in.reshape(width, LANES), (((1,), (1,)), ((), ())),
            preferred_element_type=f32,
        ).astype(bf16)
    return (grad_in[None], grad_filter, grad_proj)


def solution(mesh):
    mesh = Mesh(mesh.devices.reshape(2, 2, 2, 4, 4), SEQ + POS)
    placed = (
        P(SEQ, POS, None),
        P(SEQ, POS, None),
        P(SEQ, POS, None),
        P(None, POS),
        P(),
        P(SEQ + POS, None),
    )
    return jax.shard_map(
        on_device,
        mesh=mesh,
        in_specs=placed,
        out_specs=(P(SEQ, POS, None), P(POS, SEQ), P(SEQ + POS, None)),
        check_vma=False,
    )
```

```python
import functools
import math

import jax
import jax.numpy as jnp
from jax import lax
from jax.experimental import pallas as pl
from jax.experimental.pallas import tpu as pltpu
from jax.sharding import Mesh, PartitionSpec as P

LANES = 128
HALF = LANES // 2
GROUP = 4
f32, bf16 = jnp.float32, jnp.bfloat16


def iota(rows, axis):
    return lax.broadcasted_iota(jnp.int32, (rows, LANES), axis)


def turn(field, by):
    return pltpu.roll(field, by, 1)


def moved(field, by):
    if by == 0:
        return field
    gap = jnp.zeros((abs(by), LANES), field.dtype)
    if by > 0:
        return jnp.concatenate([gap, field[:-by]], axis=0)
    return jnp.concatenate([field[-by:], gap], axis=0)


def mirror():
    return (iota(LANES, 0) + iota(LANES, 1) == LANES - 1).astype(bf16)


def tap_rows(taps, first, before):
    same = iota(HALF, 1) >= iota(HALF, 0)
    parts = []
    for delta in range(first, first + GROUP):
        line = jnp.broadcast_to(taps[delta : delta + 1, :], (HALF, LANES))
        here = pltpu.roll(line, 0, 1, stride=1, stride_axis=0)
        parts.append(jnp.where(same, here, before).astype(bf16))
        before = here
    return jnp.concatenate(parts, axis=0), before


def correlate(field, taps, seqs, sign):
    rows, span = field.shape[0], GROUP * seqs
    low = iota(rows, 1) < HALF
    beside = moved(field, sign * seqs)
    halves = [
        jnp.where(low, field, turn(beside, HALF)),
        jnp.where(low, turn(field, HALF), beside),
    ]
    wide = [
        jnp.concatenate([h.astype(bf16), moved(h, sign * 2 * seqs).astype(bf16)], axis=1)
        for h in halves
    ]
    total = [jnp.zeros((rows, LANES), f32)] * 2
    before = jnp.zeros((HALF, LANES), f32)
    for k in range(rows // span):
        matrix, before = tap_rows(taps, k * GROUP, before)
        cut = k * span
        kept = [w[: rows - cut] if sign > 0 else w[cut:] for w in wide]
        part = jnp.dot(jnp.concatenate(kept, axis=0), matrix, preferred_element_type=f32)
        for p in range(2):
            add = part[p * (rows - cut) : (p + 1) * (rows - cut)]
            if cut:
                gap = jnp.zeros((cut, LANES), f32)
                add = jnp.concatenate([gap, add] if sign > 0 else [add, gap], axis=0)
            total[p] = total[p] + add
    across = turn(total[1], HALF)
    return total[0] + jnp.where(low, moved(across, sign * seqs), across)


def conv_kernel(seqs, skip_ref, x_ref, h_ref, y_ref):
    many = x_ref.shape[0]
    for i in range(many):
        x = x_ref[i].astype(f32)
        y = correlate(x, h_ref[i].astype(f32), seqs, 1)
        y_ref[i] = (y + x * skip_ref[pl.program_id(0) * many + i]).astype(bf16)


def back_kernel(seqs, skip_ref, d_ref, h_ref, y_ref):
    many = d_ref.shape[0]
    for i in range(many):
        d = d_ref[i].astype(f32)
        y = correlate(d, h_ref[i].astype(f32), seqs, -1)
        y_ref[i] = (y + d * skip_ref[pl.program_id(0) * many + i]).astype(bf16)


def taps_kernel(seqs, scale_ref, x_ref, d_ref, f_ref, long_ref, sum_ref):
    many, rows, _ = x_ref.shape
    blocks, span = rows // seqs, GROUP * seqs
    same = (iota(LANES, 0) == iota(LANES, 1)).astype(bf16)
    keep = iota(HALF, 0) + iota(HALF, 1) < LANES
    step = pl.program_id(0)
    for i in range(many):
        x, d = x_ref[i].astype(f32), d_ref[i].astype(f32)
        left = []
        for v in range(GROUP):
            part = moved(x, v * seqs).astype(bf16)
            part = lax.dot_general(
                same, part, (((1,), (1,)), ((), ())), preferred_element_type=f32
            ).astype(bf16)
            left.append(jnp.concatenate([part[:HALF], part[HALF:]], axis=1))
        left = jnp.concatenate(left, axis=0)
        across = turn(d, HALF)
        shifted = jnp.where(iota(rows, 1) < HALF, moved(across, -seqs), across)
        for p, part in enumerate((d, shifted)):
            long_ref[i, p, :rows, :] = part.astype(bf16)
            long_ref[i, p, rows:, :] = jnp.zeros((rows, LANES), bf16)
        after = jnp.zeros((HALF, LANES), f32)

        def outer(k):
            right = [
                jnp.concatenate(
                    [long_ref[i, p, at * span : at * span + rows, :] for p in range(2)], axis=0
                )
                for at in (k, k + 1)
            ]
            return jnp.dot(left, jnp.concatenate(right, axis=1), preferred_element_type=f32)

        steps = list(reversed(range(0, rows // span, 2)))
        ready = outer(steps[0])
        for n, k in enumerate(steps):
            now = ready
            if n + 1 < len(steps):
                ready = outer(steps[n + 1])
            for j in reversed(range(2 * GROUP)):
                at, v = j // GROUP, j % GROUP
                here = now[v * HALF : (v + 1) * HALF, at * LANES : (at + 1) * LANES]
                lined = pltpu.roll(jnp.where(keep, here, after), 0, 1, stride=1, stride_axis=0)
                delta = k * GROUP + j
                sum_ref[pl.ds((step * many + i) * blocks + delta, 1), :] = (
                    jnp.sum(lined, axis=0, keepdims=True) * scale_ref[0]
                )
                after = here

    @pl.when(step == pl.num_programs(0) - 1)
    def _():
        f_ref[...] = jnp.dot(
            sum_ref[...].astype(bf16), mirror(), preferred_element_type=f32
        ).astype(bf16)


MANY = 4
TAPS_MANY = 8


def per_channel(many, shape):
    return pl.BlockSpec((many, *shape[1:]), lambda i: (i, 0, 0))


def estimate(flops):
    return pl.CostEstimate(flops=flops, bytes_accessed=1 << 16, transcendentals=0)


def conv_call(kernel, field, taps, skip, seqs):
    chans, rows = taps.shape[0], field.shape[1]
    return pl.pallas_call(
        functools.partial(kernel, seqs),
        grid=(chans // MANY,),
        in_specs=[
            pl.BlockSpec(memory_space=pltpu.SMEM),
            per_channel(MANY, field.shape),
            per_channel(MANY, taps.shape),
        ],
        out_specs=per_channel(MANY, field.shape),
        out_shape=jax.ShapeDtypeStruct((chans, rows, LANES), bf16),
        compiler_params=pltpu.CompilerParams(vmem_limit_bytes=24 << 20),
        cost_estimate=estimate(1 << 20),
    )(skip, field, taps)


def taps_call(x, d, seqs, scale):
    chans, rows, _ = d.shape
    out = jax.ShapeDtypeStruct((chans * rows // seqs, LANES), bf16)
    return pl.pallas_call(
        functools.partial(taps_kernel, seqs),
        grid=(chans // TAPS_MANY,),
        in_specs=[
            pl.BlockSpec(memory_space=pltpu.SMEM),
            per_channel(TAPS_MANY, x.shape),
            per_channel(TAPS_MANY, d.shape),
        ],
        out_specs=pl.BlockSpec(out.shape, lambda i: (0, 0)),
        out_shape=out,
        scratch_shapes=[
            pltpu.VMEM((TAPS_MANY, 2, 2 * rows, LANES), bf16),
            pltpu.VMEM(out.shape, f32),
        ],
        compiler_params=pltpu.CompilerParams(vmem_limit_bytes=24 << 20),
        cost_estimate=estimate(1 << 20),
    )(scale, x, d).reshape(chans, rows // seqs, LANES)


def dconv_kernel(place_ref, w_ref, *refs):
    *pieces, out_ref, weight_ref = refs
    for k in range(weight_ref.shape[1] // LANES):
        weight_ref[:, k * LANES : (k + 1) * LANES] = w_ref[:, k].reshape(-1, LANES)
    flip = mirror()
    for first in range(0, len(pieces), GROUP):
        block = jnp.concatenate([piece[...] for piece in pieces[first : first + GROUP]], axis=0)
        wide = lax.dot_general(
            weight_ref[...], block, (((1,), (1,)), ((), ())), preferred_element_type=f32
        ).astype(bf16)
        for j in range(GROUP):
            part = wide[:, j * LANES : (j + 1) * LANES]
            part = jnp.dot(part, flip, preferred_element_type=f32).astype(bf16)
            out_ref[:, pl.ds(place_ref[first + j], 1)] = part.reshape(
                out_ref.shape[0], 1, *out_ref.shape[2:]
            )


def proj_kernel(place_ref, c_ref, *refs):
    *pieces, out_ref, lhs_ref = refs
    rows, width = out_ref.shape
    ahead = c_ref.shape[1] - len(pieces)
    for j in range(len(pieces)):
        part = c_ref[:, pl.ds(ahead + place_ref[j], 1)]
        lhs_ref[:, j * LANES : (j + 1) * LANES] = part.reshape(rows, LANES)
    step = 512
    for at in range(0, width, step):
        block = jnp.concatenate([piece[:, at : at + step] for piece in pieces], axis=0)
        out_ref[:, at : at + step] = jnp.dot(
            lhs_ref[...], block, preferred_element_type=f32
        ).astype(bf16)


def whole(count):
    return [pl.BlockSpec(memory_space=pltpu.VMEM)] * count


def dconv_call(place, load, pieces):
    plane, _, chans, _ = load.shape
    return pl.pallas_call(
        dconv_kernel,
        in_specs=[pl.BlockSpec(memory_space=pltpu.SMEM), *whole(1 + len(pieces))],
        out_specs=whole(1)[0],
        out_shape=jax.ShapeDtypeStruct((plane, len(pieces), chans, LANES), bf16),
        scratch_shapes=[pltpu.VMEM((plane * chans, pieces[0].shape[1]), bf16)],
        compiler_params=pltpu.CompilerParams(vmem_limit_bytes=32 << 20),
        cost_estimate=pl.CostEstimate(flops=1 << 30, bytes_accessed=6 << 20, transcendentals=0),
    )(place, load, *pieces)


def proj_call(place, conv, pieces):
    rows = conv.shape[0] * conv.shape[2]
    width = pieces[0].shape[1]
    return pl.pallas_call(
        proj_kernel,
        in_specs=[pl.BlockSpec(memory_space=pltpu.SMEM), *whole(1 + len(pieces))],
        out_specs=whole(1)[0],
        out_shape=jax.ShapeDtypeStruct((rows, width), jnp.bfloat16),
        scratch_shapes=[pltpu.VMEM((rows, len(pieces) * LANES), jnp.bfloat16)],
        compiler_params=pltpu.CompilerParams(vmem_limit_bytes=32 << 20),
        cost_estimate=pl.CostEstimate(flops=1 << 30, bytes_accessed=6 << 20, transcendentals=0),
    )(place, conv, *pieces)


SEQ = ("zl", "core")
POS = ("zh", "yh", "yl", "xh", "xl")
PLANE = ("yl", "yh", "xl", "xh")
COLUMN = ("zl", "core", "zh")


def column_pairs(step, other):
    pairs = []
    for z in range(4):
        for core in range(2):
            to, to_core = (z + step) % 4, core ^ other
            pairs.append(
                (z % 2 * 4 + core * 2 + z // 2, to % 2 * 4 + to_core * 2 + to // 2)
            )
    return pairs


def move(a, step, other=0):
    return lax.ppermute(a, COLUMN, column_pairs(step, other))


def places():
    z = 2 * lax.axis_index("zh") + lax.axis_index("zl")
    core = lax.axis_index("core")
    place = [(z + step) % 4 * 2 + (core + other) % 2 for other in (0, 1) for step in (0, 3, 1, 2)]
    return jnp.stack(place).astype(jnp.int32)


def on_device(quant_input, input_scales, out_grad, filter_taps, skip, proj_weight):
    tokens, width = quant_input.shape[1:]
    ctx, seqs, plane = (lax.axis_size(a) for a in (POS, SEQ, PLANE))
    me_dp, me_ctx = lax.axis_index(SEQ), lax.axis_index(POS)
    blocks = input_scales.shape[2]
    chans = width // (ctx * seqs)
    column = ctx * seqs // plane

    with jax.named_scope("signal"):
        signal = (
            (quant_input[0].reshape(tokens, blocks, width // blocks) * input_scales[0][:, :, None])
            .reshape(tokens, width)
            .astype(bf16)
        )
        few = chans // seqs
        parts = signal.T.reshape(seqs, ctx, seqs, few, tokens)
        taps = filter_taps.reshape(seqs, ctx, seqs, chans // seqs, tokens)
        taps = lax.dynamic_index_in_dim(taps, me_dp, 2)
        load = jnp.concatenate([parts, taps], axis=2).transpose(1, 0, 2, 3, 4)
        load = load.reshape(ctx * seqs, -1, few, LANES)
    with jax.named_scope("signal_a2a"):
        load = lax.all_to_all(load, POS + SEQ, 0, 0)
        load = load.reshape(ctx * seqs, -1, LANES)
    with jax.named_scope("signal_in"):
        x = load[:, :chans].transpose(1, 0, 2)
        h = load[:, chans:].reshape(ctx, seqs, chans // seqs, LANES).transpose(1, 2, 0, 3)
        h = h.reshape(chans, ctx, LANES)
        first = (me_dp * ctx + me_ctx) * chans
        own_skip = lax.dynamic_slice_in_dim(skip, first, chans)
    with jax.named_scope("share_cotangent"):
        own = out_grad[0]
        place = places()
        below, above, beside = move(own, 1), move(own, 3), move(own, 0, 1)
        half = tokens // 2
        far = jnp.concatenate([move(below[:half], 1), move(above[half:], 3)], axis=0)
        pieces = [own, below, above, far, beside]
        pieces += [move(a, 0, 1) for a in (below, above, far)]
    with jax.named_scope("weight_load"):
        rows = proj_weight.reshape(chans, width // LANES, LANES).transpose(1, 0, 2)
        rows = jnp.broadcast_to(rows[None], (plane, *rows.shape))
        load = jnp.pad(rows, ((0, 0), (0, column), (0, 0), (0, 0)))
        load, h = lax.optimization_barrier((load, h))
    with jax.named_scope("conv"):
        conv = conv_call(conv_kernel, x, h, own_skip, seqs)
        order = [POS.index(name) for name in PLANE]
        conv = conv.reshape(chans, ctx // plane, 2, 2, 2, 2, seqs, LANES)
        conv = conv.transpose(*(1 + at for at in order), 1, 6, 0, 7)
        conv = conv.reshape(plane, column, chans, LANES)
    with jax.named_scope("conv_a2a"):
        load = lax.dynamic_update_slice(load, conv, (0, width // LANES, 0, 0))
        load = lax.all_to_all(load, PLANE, 0, 0)
    with jax.named_scope("dconv"):
        dconv = dconv_call(place, load, pieces)
    with jax.named_scope("dconv_a2a"):
        dconv = lax.all_to_all(dconv, PLANE, 0, 0)
        dconv = dconv.reshape(2, 2, 2, 2, ctx // plane, seqs, chans, LANES)
        back = [PLANE.index(name) for name in POS[1:]]
        dconv = dconv.transpose(6, 4, *back, 5, 7).reshape(chans, ctx * seqs, LANES)
    factor = 1.0 / math.sqrt(seqs * tokens * ctx)
    with jax.named_scope("grad_proj"):
        partial = proj_call(place, load, pieces)
        partial, scale, own_skip = lax.optimization_barrier(
            (partial, jnp.full((1,), factor, f32), own_skip)
        )
    with jax.named_scope("grad_taps"):
        grad_taps = taps_call(x, dconv, seqs, scale)
        pairs = []
        for d in range(seqs):
            for c in range(ctx):
                at, x_row = (d * ctx + c) // seqs, c % seqs
                pairs.append((d * ctx + c, x_row * ctx + at))
        held = lax.ppermute(grad_taps, SEQ + POS, pairs)
    with jax.named_scope("grad_in"):
        grad_in = conv_call(back_kernel, dconv, h, own_skip, seqs).transpose(1, 0, 2)
    with jax.named_scope("grad_proj_a2a"):
        partial = lax.all_to_all(partial.reshape(plane, chans, width), PLANE, 0, 0)
        partial, held = lax.optimization_barrier((partial, held))
        grad_proj = jnp.sum(partial.astype(f32), axis=0) * factor
    with jax.named_scope("grad_in_a2a"):
        grad_in = lax.all_to_all(grad_in, POS + SEQ, 0, 0)
    with jax.named_scope("grad_filter"):
        held = held.reshape(chans, seqs, ctx // seqs, LANES).transpose(1, 0, 2, 3)
        got = []
        for k in range(seqs):
            piece = lax.dynamic_index_in_dim(held, me_dp ^ k, 0, keepdims=False)
            if k:
                piece = lax.ppermute(piece, SEQ, [(i, i ^ k) for i in range(seqs)])
            got.append(piece)
        got = jnp.stack(got)
        grad_filter = jnp.concatenate(
            [lax.dynamic_index_in_dim(got, me_dp ^ m, 0, keepdims=False) for m in range(seqs)],
            axis=0,
        )
        grad_filter = grad_filter.reshape(seqs * chans, -1).astype(f32)
        flip, grad_filter = lax.optimization_barrier((mirror(), grad_filter))
    with jax.named_scope("grad_in_out"):
        grad_in = grad_in.reshape(ctx, seqs, chans, LANES).transpose(1, 0, 2, 3)
        grad_in = lax.dot_general(
            flip, grad_in.reshape(width, LANES), (((1,), (1,)), ((), ())),
            preferred_element_type=f32,
        ).astype(bf16)
    return (grad_in[None], grad_filter, grad_proj)


def solution(mesh):
    mesh = Mesh(mesh.devices.reshape((2,) * 7), SEQ + POS)
    placed = (
        P(SEQ, POS, None),
        P(SEQ, POS, None),
        P(SEQ, POS, None),
        P(None, POS),
        P(),
        P(SEQ + POS, None),
    )
    return jax.shard_map(
        on_device,
        mesh=mesh,
        in_specs=placed,
        out_specs=(P(SEQ, POS, None), P(POS, SEQ), P(SEQ + POS, None)),
        check_vma=False,
    )
```

```python
import functools
import math

import jax
import jax.numpy as jnp
from jax import lax
from jax.experimental import pallas as pl
from jax.experimental.pallas import tpu as pltpu
from jax.sharding import Mesh, PartitionSpec as P

LANES = 128
HALF = LANES // 2
GROUP = 4
f32, bf16 = jnp.float32, jnp.bfloat16


def iota(rows, axis):
    return lax.broadcasted_iota(jnp.int32, (rows, LANES), axis)


def turn(field, by):
    return pltpu.roll(field, by, 1)


def moved(field, by):
    if by == 0:
        return field
    gap = jnp.zeros((abs(by), LANES), field.dtype)
    if by > 0:
        return jnp.concatenate([gap, field[:-by]], axis=0)
    return jnp.concatenate([field[-by:], gap], axis=0)


def mirror():
    return (iota(LANES, 0) + iota(LANES, 1) == LANES - 1).astype(bf16)


def tap_rows(taps, first, before):
    same = iota(HALF, 1) >= iota(HALF, 0)
    parts = []
    for delta in range(first, first + GROUP):
        line = jnp.broadcast_to(taps[delta : delta + 1, :], (HALF, LANES))
        here = pltpu.roll(line, 0, 1, stride=1, stride_axis=0)
        parts.append(jnp.where(same, here, before).astype(bf16))
        before = here
    return jnp.concatenate(parts, axis=0), before


def correlate(field, taps, seqs, sign):
    rows, span = field.shape[0], GROUP * seqs
    low = iota(rows, 1) < HALF
    beside = moved(field, sign * seqs)
    halves = [
        jnp.where(low, field, turn(beside, HALF)),
        jnp.where(low, turn(field, HALF), beside),
    ]
    wide = [
        jnp.concatenate([h.astype(bf16), moved(h, sign * 2 * seqs).astype(bf16)], axis=1)
        for h in halves
    ]
    total = [jnp.zeros((rows, LANES), f32)] * 2
    before = jnp.zeros((HALF, LANES), f32)
    for k in range(rows // span):
        matrix, before = tap_rows(taps, k * GROUP, before)
        cut = k * span
        kept = [w[: rows - cut] if sign > 0 else w[cut:] for w in wide]
        part = jnp.dot(jnp.concatenate(kept, axis=0), matrix, preferred_element_type=f32)
        for p in range(2):
            add = part[p * (rows - cut) : (p + 1) * (rows - cut)]
            if cut:
                gap = jnp.zeros((cut, LANES), f32)
                add = jnp.concatenate([gap, add] if sign > 0 else [add, gap], axis=0)
            total[p] = total[p] + add
    across = turn(total[1], HALF)
    return total[0] + jnp.where(low, moved(across, sign * seqs), across)


def conv_kernel(seqs, skip_ref, x_ref, h_ref, y_ref):
    many = x_ref.shape[0]
    for i in range(many):
        x = x_ref[i].astype(f32)
        y = correlate(x, h_ref[i].astype(f32), seqs, 1)
        y_ref[i] = (y + x * skip_ref[pl.program_id(0) * many + i]).astype(bf16)


def back_kernel(seqs, skip_ref, d_ref, h_ref, y_ref):
    many = d_ref.shape[0]
    for i in range(many):
        d = d_ref[i].astype(f32)
        y = correlate(d, h_ref[i].astype(f32), seqs, -1)
        y_ref[i] = (y + d * skip_ref[pl.program_id(0) * many + i]).astype(bf16)


def taps_kernel(seqs, scale_ref, x_ref, d_ref, f_ref, long_ref, sum_ref):
    many, rows, _ = x_ref.shape
    blocks, span = rows // seqs, GROUP * seqs
    same = (iota(LANES, 0) == iota(LANES, 1)).astype(bf16)
    keep = iota(HALF, 0) + iota(HALF, 1) < LANES
    step = pl.program_id(0)
    for i in range(many):
        x, d = x_ref[i].astype(f32), d_ref[i].astype(f32)
        left = []
        for v in range(GROUP):
            part = moved(x, v * seqs).astype(bf16)
            part = lax.dot_general(
                same, part, (((1,), (1,)), ((), ())), preferred_element_type=f32
            ).astype(bf16)
            left.append(jnp.concatenate([part[:HALF], part[HALF:]], axis=1))
        left = jnp.concatenate(left, axis=0)
        across = turn(d, HALF)
        shifted = jnp.where(iota(rows, 1) < HALF, moved(across, -seqs), across)
        for p, part in enumerate((d, shifted)):
            long_ref[i, p, :rows, :] = part.astype(bf16)
            long_ref[i, p, rows:, :] = jnp.zeros((rows, LANES), bf16)
        after = jnp.zeros((HALF, LANES), f32)

        def outer(k):
            right = [
                jnp.concatenate(
                    [long_ref[i, p, at * span : at * span + rows, :] for p in range(2)], axis=0
                )
                for at in (k, k + 1)
            ]
            return jnp.dot(left, jnp.concatenate(right, axis=1), preferred_element_type=f32)

        steps = list(reversed(range(0, rows // span, 2)))
        ready = outer(steps[0])
        for n, k in enumerate(steps):
            now = ready
            if n + 1 < len(steps):
                ready = outer(steps[n + 1])
            for j in reversed(range(2 * GROUP)):
                at, v = j // GROUP, j % GROUP
                here = now[v * HALF : (v + 1) * HALF, at * LANES : (at + 1) * LANES]
                lined = pltpu.roll(jnp.where(keep, here, after), 0, 1, stride=1, stride_axis=0)
                delta = k * GROUP + j
                sum_ref[pl.ds((step * many + i) * blocks + delta, 1), :] = (
                    jnp.sum(lined, axis=0, keepdims=True) * scale_ref[0]
                )
                after = here

    @pl.when(step == pl.num_programs(0) - 1)
    def _():
        f_ref[...] = jnp.dot(
            sum_ref[...].astype(bf16), mirror(), preferred_element_type=f32
        ).astype(bf16)


MANY = 8


def per_channel(many, shape):
    return pl.BlockSpec((many, *shape[1:]), lambda i: (i, 0, 0))


def estimate(flops):
    return pl.CostEstimate(flops=flops, bytes_accessed=1 << 16, transcendentals=0)


def conv_call(kernel, field, taps, skip, seqs):
    chans, rows = taps.shape[0], field.shape[1]
    return pl.pallas_call(
        functools.partial(kernel, seqs),
        grid=(chans // MANY,),
        in_specs=[
            pl.BlockSpec(memory_space=pltpu.SMEM),
            per_channel(MANY, field.shape),
            per_channel(MANY, taps.shape),
        ],
        out_specs=per_channel(MANY, field.shape),
        out_shape=jax.ShapeDtypeStruct((chans, rows, LANES), bf16),
        compiler_params=pltpu.CompilerParams(vmem_limit_bytes=24 << 20),
        cost_estimate=estimate(1 << 20),
    )(skip, field, taps)


def taps_call(x, d, seqs, scale):
    chans, rows, _ = d.shape
    out = jax.ShapeDtypeStruct((chans * rows // seqs, LANES), bf16)
    return pl.pallas_call(
        functools.partial(taps_kernel, seqs),
        grid=(chans // MANY,),
        in_specs=[
            pl.BlockSpec(memory_space=pltpu.SMEM),
            per_channel(MANY, x.shape),
            per_channel(MANY, d.shape),
        ],
        out_specs=pl.BlockSpec(out.shape, lambda i: (0, 0)),
        out_shape=out,
        scratch_shapes=[
            pltpu.VMEM((MANY, 2, 2 * rows, LANES), bf16),
            pltpu.VMEM(out.shape, f32),
        ],
        compiler_params=pltpu.CompilerParams(vmem_limit_bytes=24 << 20),
        cost_estimate=estimate(1 << 20),
    )(scale, x, d).reshape(chans, rows // seqs, LANES)


def dconv_kernel(place_ref, w_ref, *refs):
    *pieces, out_ref, weight_ref = refs
    for k in range(weight_ref.shape[1] // LANES):
        weight_ref[:, k * LANES : (k + 1) * LANES] = w_ref[:, k].reshape(-1, LANES)
    flip = mirror()
    for first in range(0, len(pieces), GROUP):
        block = jnp.concatenate([piece[...] for piece in pieces[first : first + GROUP]], axis=0)
        wide = lax.dot_general(
            weight_ref[...], block, (((1,), (1,)), ((), ())), preferred_element_type=f32
        ).astype(bf16)
        for j in range(GROUP):
            part = wide[:, j * LANES : (j + 1) * LANES]
            part = jnp.dot(part, flip, preferred_element_type=f32).astype(bf16)
            out_ref[:, pl.ds(place_ref[first + j], 1)] = part.reshape(
                out_ref.shape[0], 1, *out_ref.shape[2:]
            )


def proj_kernel(place_ref, c_ref, *refs):
    *pieces, out_ref, lhs_ref = refs
    rows, width = out_ref.shape
    ahead = c_ref.shape[1] - len(pieces)
    for j in range(len(pieces)):
        part = c_ref[:, pl.ds(ahead + place_ref[j], 1)]
        lhs_ref[:, j * LANES : (j + 1) * LANES] = part.reshape(rows, LANES)
    step = 512
    for at in range(0, width, step):
        block = jnp.concatenate([piece[:, at : at + step] for piece in pieces], axis=0)
        out_ref[:, at : at + step] = jnp.dot(
            lhs_ref[...], block, preferred_element_type=f32
        ).astype(bf16)


def load_kernel(me_ref, q_ref, scale_ref, taps_ref, out_ref):
    seqs, few = out_ref.shape[2] - 1, out_ref.shape[3]
    chans = few * seqs
    same = (iota(LANES, 0) == iota(LANES, 1)).astype(bf16)
    count = LANES // chans
    rows, cols = iota(few * count, 0), iota(few * count, 1)
    pick = (cols == rows // few * chans + rows % few + me_ref[0] * few).astype(bf16)
    blocks = q_ref.shape[1] // LANES
    for b in range(blocks):
        part = lax.dot_general(
            same, q_ref[:, b * LANES : (b + 1) * LANES], (((1,), (1,)), ((), ())),
            preferred_element_type=f32,
        )
        scale = scale_ref[pl.ds(pl.program_id(0) * blocks + b, 1), :]
        part = (part * scale).reshape(count, seqs, few, LANES)
        taps = jnp.dot(pick, taps_ref[b * LANES : (b + 1) * LANES, :], preferred_element_type=f32)
        taps = taps.reshape(count, few, LANES)
        each = blocks // out_ref.shape[1]
        for k in range(count):
            out_ref[b % each * count + k, b // each, :seqs] = part[k].astype(bf16)
            out_ref[b % each * count + k, b // each, seqs] = taps[k].astype(bf16)


def whole(count):
    return [pl.BlockSpec(memory_space=pltpu.VMEM)] * count


def dconv_call(place, load, pieces):
    plane, _, chans, _ = load.shape
    return pl.pallas_call(
        dconv_kernel,
        in_specs=[pl.BlockSpec(memory_space=pltpu.SMEM), *whole(1 + len(pieces))],
        out_specs=whole(1)[0],
        out_shape=jax.ShapeDtypeStruct((plane, len(pieces), chans, LANES), bf16),
        scratch_shapes=[pltpu.VMEM((plane * chans, pieces[0].shape[1]), bf16)],
        compiler_params=pltpu.CompilerParams(vmem_limit_bytes=32 << 20),
        cost_estimate=pl.CostEstimate(flops=1 << 30, bytes_accessed=6 << 20, transcendentals=0),
    )(place, load, *pieces)


def load_call(me, values, scales, taps, owners, seqs):
    steps = 2
    width = taps.shape[0] // steps
    few = taps.shape[0] // owners // seqs
    owners = owners // seqs
    shape = (owners, seqs, seqs + 1, few, LANES)
    load = pl.pallas_call(
        load_kernel,
        grid=(steps,),
        in_specs=[
            pl.BlockSpec(memory_space=pltpu.SMEM),
            pl.BlockSpec((values.shape[0], width), lambda i: (0, i)),
            pl.BlockSpec(scales.shape, lambda i: (0, 0)),
            pl.BlockSpec((width, LANES), lambda i: (i, 0)),
        ],
        out_specs=pl.BlockSpec((owners, seqs // steps, *shape[2:]), lambda i: (0, i, 0, 0, 0)),
        out_shape=jax.ShapeDtypeStruct(shape, bf16),
        compiler_params=pltpu.CompilerParams(vmem_limit_bytes=60 << 20),
        cost_estimate=estimate(1 << 20),
    )(me, values, scales, taps)
    return load.reshape(owners * seqs, *shape[2:])


def proj_call(place, conv, pieces):
    rows = conv.shape[0] * conv.shape[2]
    width = pieces[0].shape[1]
    return pl.pallas_call(
        proj_kernel,
        in_specs=[pl.BlockSpec(memory_space=pltpu.SMEM), *whole(1 + len(pieces))],
        out_specs=whole(1)[0],
        out_shape=jax.ShapeDtypeStruct((rows, width), jnp.bfloat16),
        scratch_shapes=[pltpu.VMEM((rows, len(pieces) * LANES), jnp.bfloat16)],
        compiler_params=pltpu.CompilerParams(vmem_limit_bytes=32 << 20),
        cost_estimate=pl.CostEstimate(flops=1 << 30, bytes_accessed=6 << 20, transcendentals=0),
    )(place, conv, *pieces)


SEQ = ("zl", "core")
POS = ("zh", "yh", "yl", "xh", "xl")
PLANE = ("yl", "yh", "xl", "xh")
COLUMN = ("zl", "core", "zh")


def column_pairs(step, other):
    pairs = []
    for z in range(4):
        for core in range(2):
            to, to_core = (z + step) % 4, core ^ other
            pairs.append(
                (z % 2 * 4 + core * 2 + z // 2, to % 2 * 4 + to_core * 2 + to // 2)
            )
    return pairs


def move(a, step, other=0):
    return lax.ppermute(a, COLUMN, column_pairs(step, other))


def places():
    z = 2 * lax.axis_index("zh") + lax.axis_index("zl")
    core = lax.axis_index("core")
    place = [(z + step) % 4 * 2 + (core + other) % 2 for other in (0, 1) for step in (0, 3, 1, 2)]
    return jnp.stack(place).astype(jnp.int32)


def on_device(quant_input, input_scales, out_grad, filter_taps, skip, proj_weight):
    tokens, width = quant_input.shape[1:]
    ctx, seqs, plane = (lax.axis_size(a) for a in (POS, SEQ, PLANE))
    me_dp, me_ctx = lax.axis_index(SEQ), lax.axis_index(POS)
    chans = width // (ctx * seqs)
    column = ctx * seqs // plane

    with jax.named_scope("signal"):
        me = jnp.full((1,), me_dp, jnp.int32)
        load = load_call(me, quant_input[0], input_scales[0].T, filter_taps, ctx * seqs, seqs)
    with jax.named_scope("signal_a2a"):
        load = lax.all_to_all(load, POS + SEQ, 0, 0)
        load = load.reshape(ctx * seqs, -1, LANES)
    with jax.named_scope("signal_in"):
        x = load[:, :chans].transpose(1, 0, 2)
        h = load[:, chans:].reshape(ctx, seqs, chans // seqs, LANES).transpose(1, 2, 0, 3)
        h = h.reshape(chans, ctx, LANES)
        first = (me_dp * ctx + me_ctx) * chans
        own_skip = lax.dynamic_slice_in_dim(skip, first, chans)
    with jax.named_scope("share_cotangent"):
        own = out_grad[0]
        place = places()
        below, above, beside = move(own, 1), move(own, 3), move(own, 0, 1)
        half = tokens // 2
        far = jnp.concatenate([move(below[:half], 1), move(above[half:], 3)], axis=0)
        pieces = [own, below, above, far, beside]
        pieces += [move(a, 0, 1) for a in (below, above, far)]
    with jax.named_scope("weight_load"):
        rows = proj_weight.reshape(chans, width // LANES, LANES).transpose(1, 0, 2)
        rows = jnp.broadcast_to(rows[None], (plane, *rows.shape))
        load = jnp.pad(rows, ((0, 0), (0, column), (0, 0), (0, 0)))
        load, h = lax.optimization_barrier((load, h))
    with jax.named_scope("conv"):
        conv = conv_call(conv_kernel, x, h, own_skip, seqs)
        order = [POS.index(name) for name in PLANE]
        conv = conv.reshape(chans, ctx // plane, 2, 2, 2, 2, seqs, LANES)
        conv = conv.transpose(*(1 + at for at in order), 1, 6, 0, 7)
        conv = conv.reshape(plane, column, chans, LANES)
    with jax.named_scope("conv_a2a"):
        load = lax.dynamic_update_slice(load, conv, (0, width // LANES, 0, 0))
        load = lax.all_to_all(load, PLANE, 0, 0)
    with jax.named_scope("dconv"):
        dconv = dconv_call(place, load, pieces)
    with jax.named_scope("dconv_a2a"):
        dconv = lax.all_to_all(dconv, PLANE, 0, 0)
        dconv = dconv.reshape(2, 2, 2, 2, ctx // plane, seqs, chans, LANES)
        back = [PLANE.index(name) for name in POS[1:]]
        dconv = dconv.transpose(6, 4, *back, 5, 7).reshape(chans, ctx * seqs, LANES)
    factor = 1.0 / math.sqrt(seqs * tokens * ctx)
    with jax.named_scope("grad_proj"):
        partial = proj_call(place, load, pieces)
        partial, scale, own_skip = lax.optimization_barrier(
            (partial, jnp.full((1,), factor, f32), own_skip)
        )
    with jax.named_scope("grad_taps"):
        grad_taps = taps_call(x, dconv, seqs, scale)
        pairs = []
        for d in range(seqs):
            for c in range(ctx):
                at, x_row = (d * ctx + c) // seqs, c % seqs
                pairs.append((d * ctx + c, x_row * ctx + at))
        held = lax.ppermute(grad_taps, SEQ + POS, pairs)
    with jax.named_scope("grad_in"):
        grad_in = conv_call(back_kernel, dconv, h, own_skip, seqs).transpose(1, 0, 2)
    with jax.named_scope("grad_proj_a2a"):
        partial = lax.all_to_all(partial.reshape(plane, chans, width), PLANE, 0, 0)
        partial, held = lax.optimization_barrier((partial, held))
        grad_proj = jnp.sum(partial.astype(f32), axis=0) * factor
    with jax.named_scope("grad_in_a2a"):
        grad_in = lax.all_to_all(grad_in, POS + SEQ, 0, 0)
    with jax.named_scope("grad_filter"):
        held = held.reshape(chans, seqs, ctx // seqs, LANES).transpose(1, 0, 2, 3)
        got = []
        for k in range(seqs):
            piece = lax.dynamic_index_in_dim(held, me_dp ^ k, 0, keepdims=False)
            if k:
                piece = lax.ppermute(piece, SEQ, [(i, i ^ k) for i in range(seqs)])
            got.append(piece)
        got = jnp.stack(got)
        grad_filter = jnp.concatenate(
            [lax.dynamic_index_in_dim(got, me_dp ^ m, 0, keepdims=False) for m in range(seqs)],
            axis=0,
        )
        grad_filter = grad_filter.reshape(seqs * chans, -1).astype(f32)
        flip, grad_filter = lax.optimization_barrier((mirror(), grad_filter))
    with jax.named_scope("grad_in_out"):
        grad_in = grad_in.reshape(ctx, seqs, chans, LANES).transpose(1, 0, 2, 3)
        grad_in = lax.dot_general(
            flip, grad_in.reshape(width, LANES), (((1,), (1,)), ((), ())),
            preferred_element_type=f32,
        ).astype(bf16)
    return (grad_in[None], grad_filter, grad_proj)


def solution(mesh):
    mesh = Mesh(mesh.devices.reshape((2,) * 7), SEQ + POS)
    placed = (
        P(SEQ, POS, None),
        P(SEQ, POS, None),
        P(SEQ, POS, None),
        P(None, POS),
        P(),
        P(SEQ + POS, None),
    )
    return jax.shard_map(
        on_device,
        mesh=mesh,
        in_specs=placed,
        out_specs=(P(SEQ, POS, None), P(POS, SEQ), P(SEQ + POS, None)),
        check_vma=False,
    )
```

```python
import functools
import math

import jax
import jax.numpy as jnp
from jax import lax
from jax.experimental import pallas as pl
from jax.experimental.pallas import tpu as pltpu
from jax.sharding import Mesh, PartitionSpec as P

LANES = 128
HALF = LANES // 2
GROUP = 4
f32, bf16 = jnp.float32, jnp.bfloat16


def iota(rows, axis):
    return lax.broadcasted_iota(jnp.int32, (rows, LANES), axis)


def turn(field, by):
    return pltpu.roll(field, by, 1)


def moved(field, by):
    if by == 0:
        return field
    gap = jnp.zeros((abs(by), LANES), field.dtype)
    if by > 0:
        return jnp.concatenate([gap, field[:-by]], axis=0)
    return jnp.concatenate([field[-by:], gap], axis=0)


def mirror():
    return (iota(LANES, 0) + iota(LANES, 1) == LANES - 1).astype(bf16)


def tap_rows(taps, first, before):
    same = iota(HALF, 1) >= iota(HALF, 0)
    parts = []
    for delta in range(first, first + GROUP):
        line = jnp.broadcast_to(taps[delta : delta + 1, :], (HALF, LANES))
        here = pltpu.roll(line, 0, 1, stride=1, stride_axis=0)
        parts.append(jnp.where(same, here, before).astype(bf16))
        before = here
    return jnp.concatenate(parts, axis=0), before


def correlate(field, taps, seqs, sign):
    rows, span = field.shape[0], GROUP * seqs
    low = iota(rows, 1) < HALF
    beside = moved(field, sign * seqs)
    halves = [
        jnp.where(low, field, turn(beside, HALF)),
        jnp.where(low, turn(field, HALF), beside),
    ]
    wide = [
        jnp.concatenate([h.astype(bf16), moved(h, sign * 2 * seqs).astype(bf16)], axis=1)
        for h in halves
    ]
    total = [jnp.zeros((rows, LANES), f32)] * 2
    before = jnp.zeros((HALF, LANES), f32)
    for k in range(rows // span):
        matrix, before = tap_rows(taps, k * GROUP, before)
        cut = k * span
        kept = [w[: rows - cut] if sign > 0 else w[cut:] for w in wide]
        part = jnp.dot(jnp.concatenate(kept, axis=0), matrix, preferred_element_type=f32)
        for p in range(2):
            add = part[p * (rows - cut) : (p + 1) * (rows - cut)]
            if cut:
                gap = jnp.zeros((cut, LANES), f32)
                add = jnp.concatenate([gap, add] if sign > 0 else [add, gap], axis=0)
            total[p] = total[p] + add
    across = turn(total[1], HALF)
    return total[0] + jnp.where(low, moved(across, sign * seqs), across)


def conv_kernel(seqs, skip_ref, x_ref, h_ref, y_ref):
    many = x_ref.shape[0]
    for i in range(many):
        x = x_ref[i].astype(f32)
        y = correlate(x, h_ref[i].astype(f32), seqs, 1)
        y_ref[i] = (y + x * skip_ref[pl.program_id(0) * many + i]).astype(bf16)


def back_kernel(seqs, skip_ref, d_ref, h_ref, y_ref):
    many = d_ref.shape[0]
    for i in range(many):
        d = d_ref[i].astype(f32)
        y = correlate(d, h_ref[i].astype(f32), seqs, -1)
        y_ref[i] = (y + d * skip_ref[pl.program_id(0) * many + i]).astype(bf16)


def taps_kernel(seqs, scale_ref, x_ref, d_ref, f_ref, long_ref, sum_ref):
    many, rows, _ = x_ref.shape
    blocks, span = rows // seqs, GROUP * seqs
    same = (iota(LANES, 0) == iota(LANES, 1)).astype(bf16)
    keep = iota(HALF, 0) + iota(HALF, 1) < LANES
    step = pl.program_id(0)
    for i in range(many):
        x, d = x_ref[i].astype(f32), d_ref[i].astype(f32)
        left = []
        for v in range(GROUP):
            part = moved(x, v * seqs).astype(bf16)
            part = lax.dot_general(
                same, part, (((1,), (1,)), ((), ())), preferred_element_type=f32
            ).astype(bf16)
            left.append(jnp.concatenate([part[:HALF], part[HALF:]], axis=1))
        left = jnp.concatenate(left, axis=0)
        across = turn(d, HALF)
        shifted = jnp.where(iota(rows, 1) < HALF, moved(across, -seqs), across)
        for p, part in enumerate((d, shifted)):
            long_ref[i, p, :rows, :] = part.astype(bf16)
            long_ref[i, p, rows:, :] = jnp.zeros((rows, LANES), bf16)
        after = jnp.zeros((HALF, LANES), f32)

        def outer(k):
            right = [
                jnp.concatenate(
                    [long_ref[i, p, at * span : at * span + rows, :] for p in range(2)], axis=0
                )
                for at in (k, k + 1)
            ]
            return jnp.dot(left, jnp.concatenate(right, axis=1), preferred_element_type=f32)

        steps = list(reversed(range(0, rows // span, 2)))
        ready = outer(steps[0])
        for n, k in enumerate(steps):
            now = ready
            if n + 1 < len(steps):
                ready = outer(steps[n + 1])
            for j in reversed(range(2 * GROUP)):
                at, v = j // GROUP, j % GROUP
                here = now[v * HALF : (v + 1) * HALF, at * LANES : (at + 1) * LANES]
                lined = pltpu.roll(jnp.where(keep, here, after), 0, 1, stride=1, stride_axis=0)
                delta = k * GROUP + j
                sum_ref[pl.ds((step * many + i) * blocks + delta, 1), :] = (
                    jnp.sum(lined, axis=0, keepdims=True) * scale_ref[0]
                )
                after = here

    @pl.when(step == pl.num_programs(0) - 1)
    def _():
        f_ref[...] = jnp.dot(
            sum_ref[...].astype(bf16), mirror(), preferred_element_type=f32
        ).astype(bf16)


MANY = 8


def per_channel(many, shape):
    return pl.BlockSpec((many, *shape[1:]), lambda i: (i, 0, 0))


def estimate(flops):
    return pl.CostEstimate(flops=flops, bytes_accessed=1 << 16, transcendentals=0)


def conv_call(kernel, field, taps, skip, seqs):
    chans, rows = taps.shape[0], field.shape[1]
    return pl.pallas_call(
        functools.partial(kernel, seqs),
        grid=(chans // MANY,),
        in_specs=[
            pl.BlockSpec(memory_space=pltpu.SMEM),
            per_channel(MANY, field.shape),
            per_channel(MANY, taps.shape),
        ],
        out_specs=per_channel(MANY, field.shape),
        out_shape=jax.ShapeDtypeStruct((chans, rows, LANES), bf16),
        compiler_params=pltpu.CompilerParams(vmem_limit_bytes=16 << 20),
        cost_estimate=estimate(1 << 20),
    )(skip, field, taps)


def taps_call(x, d, seqs, scale):
    chans, rows, _ = d.shape
    out = jax.ShapeDtypeStruct((chans * rows // seqs, LANES), bf16)
    return pl.pallas_call(
        functools.partial(taps_kernel, seqs),
        grid=(chans // MANY,),
        in_specs=[
            pl.BlockSpec(memory_space=pltpu.SMEM),
            per_channel(MANY, x.shape),
            per_channel(MANY, d.shape),
        ],
        out_specs=pl.BlockSpec(out.shape, lambda i: (0, 0)),
        out_shape=out,
        scratch_shapes=[
            pltpu.VMEM((MANY, 2, 2 * rows, LANES), bf16),
            pltpu.VMEM(out.shape, f32),
        ],
        compiler_params=pltpu.CompilerParams(vmem_limit_bytes=16 << 20),
        cost_estimate=estimate(1 << 20),
    )(scale, x, d).reshape(chans, rows // seqs, LANES)


def dconv_kernel(place_ref, w_ref, *refs):
    *pieces, out_ref, weight_ref = refs
    for k in range(weight_ref.shape[1] // LANES):
        weight_ref[:, k * LANES : (k + 1) * LANES] = w_ref[:, k].reshape(-1, LANES)
    flip = mirror()
    for first in range(0, len(pieces), GROUP):
        block = jnp.concatenate([piece[...] for piece in pieces[first : first + GROUP]], axis=0)
        wide = lax.dot_general(
            weight_ref[...], block, (((1,), (1,)), ((), ())), preferred_element_type=f32
        ).astype(bf16)
        for j in range(GROUP):
            part = wide[:, j * LANES : (j + 1) * LANES]
            part = jnp.dot(part, flip, preferred_element_type=f32).astype(bf16)
            out_ref[:, pl.ds(place_ref[first + j], 1)] = part.reshape(
                out_ref.shape[0], 1, *out_ref.shape[2:]
            )


def proj_kernel(place_ref, c_ref, *refs):
    *pieces, out_ref, lhs_ref = refs
    rows, width = out_ref.shape
    ahead = c_ref.shape[1] - len(pieces)
    for j in range(len(pieces)):
        part = c_ref[:, pl.ds(ahead + place_ref[j], 1)]
        lhs_ref[:, j * LANES : (j + 1) * LANES] = part.reshape(rows, LANES)
    step = 512
    for at in range(0, width, step):
        block = jnp.concatenate([piece[:, at : at + step] for piece in pieces], axis=0)
        out_ref[:, at : at + step] = jnp.dot(
            lhs_ref[...], block, preferred_element_type=f32
        ).astype(bf16)


def load_kernel(me_ref, q_ref, scale_ref, taps_ref, out_ref):
    seqs, few = out_ref.shape[2] - 1, out_ref.shape[3]
    chans = few * seqs
    same = (iota(LANES, 0) == iota(LANES, 1)).astype(bf16)
    count = LANES // chans
    rows, cols = iota(few * count, 0), iota(few * count, 1)
    pick = (cols == rows // few * chans + rows % few + me_ref[0] * few).astype(bf16)
    blocks = q_ref.shape[1] // LANES
    for b in range(blocks):
        part = lax.dot_general(
            same, q_ref[:, b * LANES : (b + 1) * LANES], (((1,), (1,)), ((), ())),
            preferred_element_type=f32,
        )
        scale = scale_ref[pl.ds(pl.program_id(0) * blocks + b, 1), :]
        part = (part * scale).reshape(count, seqs, few, LANES)
        taps = jnp.dot(pick, taps_ref[b * LANES : (b + 1) * LANES, :], preferred_element_type=f32)
        taps = taps.reshape(count, few, LANES)
        each = blocks // out_ref.shape[1]
        for k in range(count):
            out_ref[b % each * count + k, b // each, :seqs] = part[k].astype(bf16)
            out_ref[b % each * count + k, b // each, seqs] = taps[k].astype(bf16)


def whole(count):
    return [pl.BlockSpec(memory_space=pltpu.VMEM)] * count


def dconv_call(place, load, pieces):
    plane, _, chans, _ = load.shape
    return pl.pallas_call(
        dconv_kernel,
        in_specs=[pl.BlockSpec(memory_space=pltpu.SMEM), *whole(1 + len(pieces))],
        out_specs=whole(1)[0],
        out_shape=jax.ShapeDtypeStruct((plane, len(pieces), chans, LANES), bf16),
        scratch_shapes=[pltpu.VMEM((plane * chans, pieces[0].shape[1]), bf16)],
        compiler_params=pltpu.CompilerParams(vmem_limit_bytes=16 << 20),
        cost_estimate=pl.CostEstimate(flops=1 << 30, bytes_accessed=6 << 20, transcendentals=0),
    )(place, load, *pieces)


def load_call(me, values, scales, taps, owners, seqs):
    steps = 2
    width = taps.shape[0] // steps
    few = taps.shape[0] // owners // seqs
    owners = owners // seqs
    shape = (owners, seqs, seqs + 1, few, LANES)
    load = pl.pallas_call(
        load_kernel,
        grid=(steps,),
        in_specs=[
            pl.BlockSpec(memory_space=pltpu.SMEM),
            pl.BlockSpec((values.shape[0], width), lambda i: (0, i)),
            pl.BlockSpec(scales.shape, lambda i: (0, 0)),
            pl.BlockSpec((width, LANES), lambda i: (i, 0)),
        ],
        out_specs=pl.BlockSpec((owners, seqs // steps, *shape[2:]), lambda i: (0, i, 0, 0, 0)),
        out_shape=jax.ShapeDtypeStruct(shape, bf16),
        compiler_params=pltpu.CompilerParams(vmem_limit_bytes=60 << 20),
        cost_estimate=estimate(1 << 20),
    )(me, values, scales, taps)
    return load.reshape(owners * seqs, *shape[2:])


def proj_call(place, conv, pieces):
    rows = conv.shape[0] * conv.shape[2]
    width = pieces[0].shape[1]
    return pl.pallas_call(
        proj_kernel,
        in_specs=[pl.BlockSpec(memory_space=pltpu.SMEM), *whole(1 + len(pieces))],
        out_specs=whole(1)[0],
        out_shape=jax.ShapeDtypeStruct((rows, width), jnp.bfloat16),
        scratch_shapes=[pltpu.VMEM((rows, len(pieces) * LANES), jnp.bfloat16)],
        compiler_params=pltpu.CompilerParams(vmem_limit_bytes=16 << 20),
        cost_estimate=pl.CostEstimate(flops=1 << 30, bytes_accessed=6 << 20, transcendentals=0),
    )(place, conv, *pieces)


SEQ = ("zl", "core")
POS = ("zh", "yh", "yl", "xh", "xl")
PLANE = ("yl", "yh", "xl", "xh")
COLUMN = ("zl", "core", "zh")


def column_pairs(step, other):
    pairs = []
    for z in range(4):
        for core in range(2):
            to, to_core = (z + step) % 4, core ^ other
            pairs.append(
                (z % 2 * 4 + core * 2 + z // 2, to % 2 * 4 + to_core * 2 + to // 2)
            )
    return pairs


def move(a, step, other=0):
    return lax.ppermute(a, COLUMN, column_pairs(step, other))


def places():
    z = 2 * lax.axis_index("zh") + lax.axis_index("zl")
    core = lax.axis_index("core")
    place = [(z + step) % 4 * 2 + (core + other) % 2 for other in (0, 1) for step in (0, 3, 1, 2)]
    return jnp.stack(place).astype(jnp.int32)


def on_device(quant_input, input_scales, out_grad, filter_taps, skip, proj_weight):
    tokens, width = quant_input.shape[1:]
    ctx, seqs, plane = (lax.axis_size(a) for a in (POS, SEQ, PLANE))
    me_dp, me_ctx = lax.axis_index(SEQ), lax.axis_index(POS)
    chans = width // (ctx * seqs)
    column = ctx * seqs // plane

    with jax.named_scope("signal"):
        me = jnp.full((1,), me_dp, jnp.int32)
        load = load_call(me, quant_input[0], input_scales[0].T, filter_taps, ctx * seqs, seqs)
    with jax.named_scope("signal_a2a"):
        load = lax.all_to_all(load, POS + SEQ, 0, 0)
        load = load.reshape(ctx * seqs, -1, LANES)
    with jax.named_scope("signal_in"):
        x = load[:, :chans].transpose(1, 0, 2)
        h = load[:, chans:].reshape(ctx, seqs, chans // seqs, LANES).transpose(1, 2, 0, 3)
        h = h.reshape(chans, ctx, LANES)
        first = (me_dp * ctx + me_ctx) * chans
        own_skip = lax.dynamic_slice_in_dim(skip, first, chans)
    with jax.named_scope("share_cotangent"):
        own = out_grad[0]
        place = places()
        below, above, beside = move(own, 1), move(own, 3), move(own, 0, 1)
        half = tokens // 2
        far = jnp.concatenate([move(below[:half], 1), move(above[half:], 3)], axis=0)
        pieces = [own, below, above, far, beside]
        pieces += [move(a, 0, 1) for a in (below, above, far)]
    with jax.named_scope("weight_load"):
        rows = proj_weight.reshape(chans, width // LANES, LANES).transpose(1, 0, 2)
        rows = jnp.broadcast_to(rows[None], (plane, *rows.shape))
        load = jnp.pad(rows, ((0, 0), (0, column), (0, 0), (0, 0)))
        load, h = lax.optimization_barrier((load, h))
    with jax.named_scope("conv"):
        conv = conv_call(conv_kernel, x, h, own_skip, seqs)
        order = [POS.index(name) for name in PLANE]
        conv = conv.reshape(chans, ctx // plane, 2, 2, 2, 2, seqs, LANES)
        conv = conv.transpose(*(1 + at for at in order), 1, 6, 0, 7)
        conv = conv.reshape(plane, column, chans, LANES)
    with jax.named_scope("conv_a2a"):
        load = lax.dynamic_update_slice(load, conv, (0, width // LANES, 0, 0))
        load = lax.all_to_all(load, PLANE, 0, 0)
    with jax.named_scope("dconv"):
        dconv = dconv_call(place, load, pieces)
    with jax.named_scope("dconv_a2a"):
        dconv = lax.all_to_all(dconv, PLANE, 0, 0)
        dconv = dconv.reshape(2, 2, 2, 2, ctx // plane, seqs, chans, LANES)
        back = [PLANE.index(name) for name in POS[1:]]
        dconv = dconv.transpose(6, 4, *back, 5, 7).reshape(chans, ctx * seqs, LANES)
    factor = 1.0 / math.sqrt(seqs * tokens * ctx)
    with jax.named_scope("grad_proj"):
        partial = proj_call(place, load, pieces)
        partial, scale, own_skip = lax.optimization_barrier(
            (partial, jnp.full((1,), factor, f32), own_skip)
        )
    with jax.named_scope("grad_taps"):
        grad_taps = taps_call(x, dconv, seqs, scale)
        pairs = []
        for d in range(seqs):
            for c in range(ctx):
                at, x_row = (d * ctx + c) // seqs, c % seqs
                pairs.append((d * ctx + c, x_row * ctx + at))
        held = lax.ppermute(grad_taps, SEQ + POS, pairs)
    with jax.named_scope("grad_in"):
        grad_in = conv_call(back_kernel, dconv, h, own_skip, seqs).transpose(1, 0, 2)
    with jax.named_scope("grad_proj_a2a"):
        partial = lax.all_to_all(partial.reshape(plane, chans, width), PLANE, 0, 0)
        partial, held = lax.optimization_barrier((partial, held))
        grad_proj = jnp.sum(partial.astype(f32), axis=0) * factor
    with jax.named_scope("grad_in_a2a"):
        grad_in = lax.all_to_all(grad_in, POS + SEQ, 0, 0)
    with jax.named_scope("grad_filter"):
        held = held.reshape(chans, seqs, ctx // seqs, LANES).transpose(1, 0, 2, 3)
        got = []
        for k in range(seqs):
            piece = lax.dynamic_index_in_dim(held, me_dp ^ k, 0, keepdims=False)
            if k:
                piece = lax.ppermute(piece, SEQ, [(i, i ^ k) for i in range(seqs)])
            got.append(piece)
        got = jnp.stack(got)
        grad_filter = jnp.concatenate(
            [lax.dynamic_index_in_dim(got, me_dp ^ m, 0, keepdims=False) for m in range(seqs)],
            axis=0,
        )
        grad_filter = grad_filter.reshape(seqs * chans, -1).astype(f32)
        flip, grad_filter = lax.optimization_barrier((mirror(), grad_filter))
    with jax.named_scope("grad_in_out"):
        grad_in = grad_in.reshape(ctx, seqs, chans, LANES).transpose(1, 0, 2, 3)
        grad_in = lax.dot_general(
            flip, grad_in.reshape(width, LANES), (((1,), (1,)), ((), ())),
            preferred_element_type=f32,
        ).astype(bf16)
    return (grad_in[None], grad_filter, grad_proj)


def solution(mesh):
    mesh = Mesh(mesh.devices.reshape((2,) * 7), SEQ + POS)
    placed = (
        P(SEQ, POS, None),
        P(SEQ, POS, None),
        P(SEQ, POS, None),
        P(None, POS),
        P(),
        P(SEQ + POS, None),
    )
    return jax.shard_map(
        on_device,
        mesh=mesh,
        in_specs=placed,
        out_specs=(P(SEQ, POS, None), P(POS, SEQ), P(SEQ + POS, None)),
        check_vma=False,
    )
```
